256 devices in a mesh: tm: 16 (over z, core), space: 16 (over y, x).
Axes of the slice: x: 4, y: 4, z: 8, core: 2. Of those that a mesh axis runs over, the one named last changes fastest.
Arguments:
- volumes: float32 [16, 64, 512, 128], P('tm', 'space'), may hold values from -12 to 12
Outputs:
- corrected: float32 [16, 64, 512, 128], P('tm', 'space')
- shifts: float32 [16, 3], P('tm')
The draws below stay inside these ranges and needn't reach their ends.
All inputs are finite; a program needn't handle non-finite values.
Results may differ from the reference program's by a relative error of at most 0.0003.
Values sent between devices are 32-bit elements; how exact they have to be, the bound alone decides.
A program may use at most 64 MiB of HBM per device.

```python
import math
import jax
import jax.numpy as jnp
from jax import lax

X = 512
Y = 128
Z = 64
ITERS = 2
TIMES = 16


def draw_volumes(key, part):
    structure = jax.random.normal(jax.random.fold_in(key, 11), (Z, X, Y), jnp.float32)
    noise_field = jax.random.normal(jax.random.fold_in(key, 12), (TIMES, Z, X, Y), jnp.float32)
    drift_steps = jax.random.randint(jax.random.fold_in(key, 13), (TIMES, 3), -2, 3)
    jitter = jax.random.uniform(jax.random.fold_in(key, 14), (TIMES,), jnp.float32, 0.6, 1.4)
    ramp_pos = jnp.arange(TIMES, dtype=jnp.float32) / max(TIMES - 1, 1)
    bright = jnp.exp(-math.log(3.0) * ramp_pos) * jitter

    def place_one(offsets):
        return jnp.roll(structure, (offsets[0], offsets[1], offsets[2]), axis=(0, 1, 2))
    rolled = jax.vmap(place_one)(drift_steps)
    volumes = bright[:, None, None, None] * rolled + 0.5 * noise_field
    return jnp.clip(volumes, -12.0, 12.0)


def setup_inputs(seed: int = 0) -> dict:
    seeds = jax.random.split(jax.random.key(seed), 2)
    return {
        "volumes": draw_volumes(jax.random.fold_in(seeds[1], 71), 0),
    }


sharpness = 256.0
floor_share = 0.05


def signed_freq(length):
    indices = jnp.arange(length, dtype=jnp.int32)
    wrapped = jnp.where(indices < length // 2, indices, indices - length)
    return jnp.where(indices == length // 2, 0, wrapped).astype(jnp.float32)


def centred(length):
    indices = jnp.arange(length, dtype=jnp.int32)
    return ((indices + length // 2) % length - length // 2).astype(jnp.float32)


def register(spectrum, template):
    product = spectrum * jnp.conj(template)
    magnitude = jnp.abs(product)
    whitened = product / jnp.maximum(magnitude, floor_share * (Z * X * Y))
    correlation = jnp.real(jnp.fft.ifftn(whitened))
    scores = sharpness * correlation
    weights = jnp.exp(scores - jnp.max(scores))
    weight_sum = jnp.sum(weights)
    moment_z = jnp.sum(jnp.sum(weights, axis=(1, 2)) * centred(Z))
    moment_x = jnp.sum(jnp.sum(weights, axis=(0, 2)) * centred(X))
    moment_y = jnp.sum(jnp.sum(weights, axis=(0, 1)) * centred(Y))
    shifts = jnp.stack([moment_z, moment_x, moment_y]) / weight_sum
    phases = (2.0 * math.pi) * (signed_freq(Z)[:, None, None] * (shifts[0] / Z)
                                + signed_freq(X)[None, :, None] * (shifts[1] / X)
                                + signed_freq(Y)[None, None, :] * (shifts[2] / Y))
    shifted = spectrum * (jnp.cos(phases) + 1j * jnp.sin(phases))
    return shifts, shifted


def reference(volumes):
    spectra = jnp.fft.fftn(volumes, axes=(1, 2, 3))
    template = jnp.mean(spectra, axis=0)
    for iteration in range(ITERS):
        shifts, shifted = lax.map(lambda spectrum: register(spectrum, template), spectra)
        template = jnp.mean(shifted, axis=0)
    corrected = jnp.real(jnp.fft.ifftn(shifted, axes=(1, 2, 3))).astype(jnp.float32)
    return corrected, shifts.astype(jnp.float32)
```

```python
import functools
import math

import jax
import jax.numpy as jnp
import ml_dtypes
import numpy as np
from jax import lax
from jax.experimental import pallas as pl
from jax.experimental.pallas import tpu as pltpu
from jax.sharding import PartitionSpec as P

X = 512
Y = 128
Z = 64
ITERS = 2
FRAMES = 16
SHARPNESS = 256.0
FLOOR = 0.05 * (X * Y * Z)

SPACE = 16
CHIPS = 8
SLABS = Z // SPACE
SLOTS = X // 2 // SPACE
ROWS = SPACE * SLOTS * 8
MSG = SLOTS * 8
UNIT = 2 * Z + 8
NQ = 4
PART = MSG // NQ
PAIRS = SLOTS // 2 // NQ
MESH = pl.DeviceIdType.MESH
F32 = jnp.float32
BF16 = jnp.bfloat16


def tables():
    def angles(n, rows, columns):
        return 2.0 * np.pi * ((rows[:, None] * columns[None, :]) % n) / n

    half = X // 2
    a = angles(X, np.arange(half), np.arange(X))
    sign = (-1.0) ** np.arange(X)
    cos_x, sin_x = np.cos(a), np.sin(a)
    im = -sin_x
    im[0] = sign
    forward_x = np.concatenate([cos_x, im])
    weight = np.full((X, 1), 2.0)
    weight[0] = weight[half] = 1.0
    inverse_x = (forward_x * weight).T / (X * Y * Z)

    a = angles(Y, np.arange(Y), np.arange(Y))
    c, s = np.cos(a), np.sin(a)
    forward_y = np.block([[c, -s], [s, c]])
    inverse_y = np.block([[c, s], [-s, c]])

    a = angles(Z, np.arange(Z), np.arange(Z))
    c, s = np.cos(a), np.sin(a)
    forward_z = np.block([[c, s], [-s, c]])
    inverse_z = np.block([[c, -s], [s, c]])
    order = np.arange(2 * Z).reshape(2, SPACE, SLABS).transpose(1, 0, 2).reshape(-1)
    forward_z = forward_z[:, order]
    inverse_z = inverse_z[order, :]

    out = []
    for table in (forward_x, inverse_x, forward_y, inverse_y, forward_z, inverse_z):
        high = table.astype(np.float32).astype(ml_dtypes.bfloat16)
        low = (table - high.astype(np.float64)).astype(np.float32).astype(ml_dtypes.bfloat16)
        out += [high, low]
    return out


def split(value):
    high = value.astype(BF16)
    return high, (value - high.astype(F32)).astype(BF16)


def dot(a, b):
    return jnp.dot(a, b, preferred_element_type=F32)


def table_dot(high, low, data):
    data_high, data_low = split(data)
    return dot(high, data_high) + (dot(high, data_low) + dot(low, data_high))


def dot_table(data, high, low):
    data_high, data_low = split(data)
    return dot(data_high, high) + (dot(data_low, high) + dot(data_high, low))


def rows_of(start, count):
    return pl.ds(pl.multiple_of(start, 8), count)


def signed(index, n):
    wrapped = jnp.where(index < n // 2, index, index - n)
    return jnp.where(index == n // 2, 0, wrapped).astype(F32)


def kernel(
    v_ref, fxh, fxl, ixh, ixl, fyh, fyl, iyh, iyl, fzh, fzl, izh, izl,
    out_ref, shift_ref,
    send_f, recv_f, spec, moved, other, pair, ring_r, ring_l, sent_r, sent_l, tmpl,
    send_i, recv_i, scores, stats_out, stats_in, ramp_zy, ramp_x,
    fwd_send, fwd_recv, inv_send, inv_recv, st_send, st_recv,
    oc_send, oc_recv, rr_send, rr_recv, rl_send, rl_recv,
    gr_send, gr_recv, gl_send, gl_recv, go_send, go_recv,
):
    s = lax.axis_index("space")
    t = lax.axis_index("tm")
    core = t % 2
    chip = t // 2
    mate = chip * 2 + 1 - core
    right = ((chip + 1) % CHIPS) * 2 + core
    left = ((chip + CHIPS - 1) % CHIPS) * 2 + core

    barrier = pltpu.get_barrier_semaphore()

    def greet(i, carry):
        pl.semaphore_signal(barrier, inc=1, device_id={"space": (s + i) % SPACE}, device_id_type=MESH)
        return carry

    lax.fori_loop(1, SPACE, greet, 0)
    for member in (mate, right, left):
        pl.semaphore_signal(barrier, inc=1, device_id={"tm": member}, device_id_type=MESH)

    row = lax.broadcasted_iota(jnp.int32, (2 * Z, 128), 0)
    first_part = (row // SLABS) % 2 == 0

    def to_space(source, start, target, target_start, send_sem, recv_sem, device, count):
        return pltpu.make_async_remote_copy(
            src_ref=source.at[rows_of(start, count)],
            dst_ref=target.at[rows_of(target_start, count)],
            send_sem=send_sem,
            recv_sem=recv_sem,
            device_id={"space": device},
            device_id_type=MESH,
        )

    for z in range(0, SLABS, 2):
        data = jnp.concatenate([v_ref[z], v_ref[z + 1]], axis=1)
        result = table_dot(fxh[...], fxl[...], data)
        for i in range(2):
            for part in range(2):
                send_f[pl.ds(part * SLABS + z + i, X // 2, stride=8), :] = result[
                    part * (X // 2) : (part + 1) * (X // 2), i * 128 : (i + 1) * 128
                ]

    pl.semaphore_wait(barrier, SPACE + 2)

    def exchange_part(source, target, send_sem, recv_sem, q):
        def one(i, carry):
            d = (s + i) % SPACE
            to_space(
                source, d * MSG + q * PART, target, s * MSG + q * PART,
                send_sem.at[q, d], recv_sem.at[q, s], d, PART,
            ).start()
            return carry

        lax.fori_loop(1, SPACE, one, 0)
        mine = rows_of(s * MSG + q * PART, PART)
        target[mine, :] = source[mine, :]

    def wait_part(source, target, send_sem, recv_sem, q):
        def one(i, carry):
            d = (s + i) % SPACE
            to_space(
                source, d * MSG + q * PART, target, d * MSG + q * PART,
                send_sem.at[q, d], recv_sem.at[q, d], d, PART,
            ).wait_recv()
            return carry

        lax.fori_loop(1, SPACE, one, 0)

    def wait_sent(source, target, send_sem, recv_sem, q):
        def one(i, carry):
            d = (s + i) % SPACE
            to_space(
                source, d * MSG + q * PART, target, s * MSG + q * PART,
                send_sem.at[q, d], recv_sem.at[q, s], d, PART,
            ).wait_send()
            return carry

        lax.fori_loop(1, SPACE, one, 0)

    def send_all(q, carry):
        exchange_part(send_f, recv_f, fwd_send, fwd_recv, q)
        return carry

    lax.fori_loop(0, NQ, send_all, 0)

    def load_slot(j):
        return jnp.concatenate([recv_f[rows_of(d * MSG + j * 8, 8), :] for d in range(SPACE)], axis=0)

    def complex_rows(value):
        return jnp.concatenate([value[:Z], value[Z:]], axis=1)

    def part_rows(value):
        return jnp.concatenate([value[:, :128], value[:, 128:]], axis=0)

    def spectrum_pair(i, carry):
        j = 2 * i
        keep = jnp.where(first_part, 1.0, jnp.where(s + j == 0, 0.0, 1.0))
        data = jnp.concatenate([load_slot(j) * keep, load_slot(j + 1)], axis=1)
        zed = table_dot(fzh[...], fzl[...], data)
        lines = jnp.concatenate([complex_rows(zed[:, :128]), complex_rows(zed[:, 128:])], axis=0)
        freq = dot_table(lines, fyh[...], fyl[...])
        spec[j, 0 : 2 * Z, :] = part_rows(freq[:Z])
        spec[j + 1, 0 : 2 * Z, :] = part_rows(freq[Z:])
        return carry

    def forward_part(q, carry):
        wait_part(send_f, recv_f, fwd_send, fwd_recv, q)
        return lax.fori_loop(q * PAIRS, (q + 1) * PAIRS, spectrum_pair, carry)

    lax.fori_loop(0, NQ, forward_part, 0)

    slot = load_slot(0)
    slot = jnp.concatenate([slot[SLABS:], slot[:SLABS]], axis=0)
    slot = slot * jnp.where(first_part, jnp.where(s == 0, 1.0, 0.0), 0.0)
    freq = dot_table(complex_rows(table_dot(fzh[...], fzl[...], slot)), fyh[...], fyl[...])
    freq = part_rows(freq)
    for u in range(SLOTS):
        spec[u, 2 * Z :, :] = freq[8 * u : 8 * u + 8]

    base = core * CHIPS
    sends = []

    def to_tm(source, target, send_sem, recv_sem, device):
        return pltpu.make_async_remote_copy(
            src_ref=source,
            dst_ref=target,
            send_sem=send_sem,
            recv_sem=recv_sem,
            device_id={"tm": device},
            device_id_type=MESH,
        )

    def start(copy):
        copy.start()
        sends.append(copy)

    def template_sum(it, source):
        copy = to_tm(
            source.at[pl.ds((1 - core) * CHIPS, CHIPS)], other.at[it], oc_send.at[it], oc_recv.at[it], mate
        )
        start(copy)
        copy.wait_recv()

        def add(u, carry):
            pair[it, u] = source[base + u] + other[it, u]
            return carry

        lax.fori_loop(0, CHIPS, add, 0)
        for k in range(4):
            unit = (chip + 4 - k) % CHIPS
            if k == 0:
                outgoing = pair.at[it, unit]
            else:
                to_tm(sent_r.at[it, k], ring_r.at[it, k - 1], rr_send.at[it, k - 1], rr_recv.at[it, k - 1], left).wait_recv()
                sent_r[it, k] = pair[it, unit] + ring_r[it, k - 1]
                outgoing = sent_r.at[it, k]
            start(to_tm(outgoing, ring_r.at[it, k], rr_send.at[it, k], rr_recv.at[it, k], right))
            if k < 3:
                unit = (chip + CHIPS - 3 + k) % CHIPS
                if k == 0:
                    outgoing = pair.at[it, unit]
                else:
                    to_tm(sent_l.at[it, k], ring_l.at[it, k - 1], rl_send.at[it, k - 1], rl_recv.at[it, k - 1], right).wait_recv()
                    sent_l[it, k] = pair[it, unit] + ring_l[it, k - 1]
                    outgoing = sent_l.at[it, k]
                start(to_tm(outgoing, ring_l.at[it, k], rl_send.at[it, k], rl_recv.at[it, k], left))
        to_tm(ring_r.at[it, 3], ring_r.at[it, 3], rr_send.at[it, 3], rr_recv.at[it, 3], left).wait_recv()
        to_tm(ring_l.at[it, 2], ring_l.at[it, 2], rl_send.at[it, 2], rl_recv.at[it, 2], right).wait_recv()
        tmpl[it, base + chip] = (pair[it, chip] + (ring_r[it, 3] + ring_l[it, 2])) * (1.0 / FRAMES)

        def to_mate(unit):
            ref = tmpl.at[it, base + unit]
            start(to_tm(ref, ref, go_send.at[it, unit], go_recv.at[it, unit], mate))

        for k in range(4):
            unit = (chip + CHIPS - k) % CHIPS
            ref = tmpl.at[it, base + unit]
            if k > 0:
                to_tm(ref, ref, gr_send.at[it, k - 1], gr_recv.at[it, k - 1], left).wait_recv()
            start(to_tm(ref, ref, gr_send.at[it, k], gr_recv.at[it, k], right))
            if k < 3:
                unit_l = (chip + k) % CHIPS
                ref_l = tmpl.at[it, base + unit_l]
                if k > 0:
                    to_tm(ref_l, ref_l, gl_send.at[it, k - 1], gl_recv.at[it, k - 1], right).wait_recv()
                start(to_tm(ref_l, ref_l, gl_send.at[it, k], gl_recv.at[it, k], left))
                if k > 0:
                    to_mate(unit_l)
            to_mate(unit)
        unit = (chip + 4) % CHIPS
        ref = tmpl.at[it, base + unit]
        to_tm(ref, ref, gr_send.at[it, 3], gr_recv.at[it, 3], left).wait_recv()
        to_mate(unit)
        unit = (chip + 3) % CHIPS
        ref = tmpl.at[it, base + unit]
        to_tm(ref, ref, gl_send.at[it, 2], gl_recv.at[it, 2], right).wait_recv()
        to_mate(unit)
        for u in range(CHIPS):
            ref = tmpl.at[it, (1 - core) * CHIPS + u]
            to_tm(ref, ref, go_send.at[it, u], go_recv.at[it, u], mate).wait_recv()

    def whiten(f_re, f_im, t_re, t_im):
        p_re = f_re * t_re + f_im * t_im
        p_im = f_im * t_re - f_re * t_im
        scale = lax.rsqrt(jnp.maximum(p_re * p_re + p_im * p_im, FLOOR * FLOOR))
        return p_re * scale, p_im * scale

    def slot_of(ref, j):
        return ref[j, 0:Z, :], ref[j, Z : 2 * Z, :]

    def last_slot(ref):
        value = jnp.concatenate([ref[u, 2 * Z :, :] for u in range(SLOTS)], axis=0)
        return value[:Z], value[Z:]

    def inverse(n, slot_values, last_values):
        def back(values):
            lines = [jnp.concatenate([re, im], axis=1) for re, im in values]
            lines = dot_table(jnp.concatenate(lines, axis=0), iyh[...], iyl[...])
            planes = [part_rows(lines[i * Z : (i + 1) * Z]) for i in range(len(values))]
            return table_dot(izh[...], izl[...], jnp.concatenate(planes, axis=1))

        last = back([last_values()])
        last = jnp.concatenate([last[2 * Z - SLABS :], last[: 2 * Z - SLABS]], axis=0)

        def pair_back(i, carry):
            j = 2 * i
            planes = back([slot_values(j), slot_values(j + 1)])
            keep = jnp.where(first_part, 1.0, jnp.where(s + j == 0, 0.0, 1.0))
            values = (planes[:, :128] * keep + last * (1.0 - keep), planes[:, 128:])
            for k in range(2):
                for d in range(SPACE):
                    send_i[n, rows_of(d * MSG + (j + k) * 8, 8), :] = values[k][8 * d : 8 * d + 8]
            return carry

        source, target, send_sem, recv_sem = send_i.at[n], recv_i.at[n], inv_send.at[n], inv_recv.at[n]

        def part_back(q, carry):
            lax.fori_loop(q * PAIRS, (q + 1) * PAIRS, pair_back, 0)
            exchange_part(source, target, send_sem, recv_sem, q)
            return carry

        lax.fori_loop(0, NQ, part_back, 0)

        def part_wait(q, carry):
            wait_part(source, target, send_sem, recv_sem, q)
            return carry

        lax.fori_loop(0, NQ, part_wait, 0)

    def cells(n, z):
        columns = []
        for i in range(2):
            parts = [
                recv_i[n, pl.ds(part * SLABS + z + i, X // 2, stride=8), :] for part in range(2)
            ]
            columns.append(jnp.concatenate(parts, axis=0))
        return table_dot(ixh[...], ixl[...], jnp.concatenate(columns, axis=1))

    lane = lax.broadcasted_iota(jnp.int32, (1, 128), 1)

    def centroid(it):
        top = jnp.full((8, 128), -jnp.inf, F32)
        for z in range(0, SLABS, 2):
            value = cells(it, z) * SHARPNESS
            for i in range(2):
                plane = value[:, i * 128 : (i + 1) * 128]
                scores[z + i] = plane
                top = jnp.maximum(top, jnp.max(plane.reshape(X // 8, 8, 128), axis=0))
        top = jnp.max(jnp.max(top, axis=0, keepdims=True), axis=1, keepdims=True)
        step = 128
        x_row = lax.broadcasted_iota(jnp.int32, (step, 128), 0)
        zero = jnp.zeros((8, 128), F32)

        def weigh(i, carry):
            total, by_z, by_x = carry
            z, x = i // (X // step), (i % (X // step)) * step
            weights = jnp.exp(scores[z, rows_of(x, step), :] - top)
            x_at = ((x + x_row + X // 2) % X - X // 2).astype(F32)
            z_at = ((s * SLABS + z + Z // 2) % Z - Z // 2).astype(F32)
            here = jnp.sum(weights.reshape(step // 8, 8, 128), axis=0)
            by_x = by_x + jnp.sum((weights * x_at).reshape(step // 8, 8, 128), axis=0)
            return total + here, by_z + here * z_at, by_x

        total, by_z, by_x = lax.fori_loop(0, SLABS * X // step, weigh, (zero, zero, zero))
        y_at = ((lane + Y // 2) % Y - Y // 2).astype(F32)
        sums = [jnp.sum(value, axis=0, keepdims=True) for value in (total, by_z, by_x)]
        rows = [jnp.broadcast_to(top, (1, 128))] + sums + [sums[0] * y_at, jnp.zeros((3, 128), F32)]
        tile = jnp.concatenate(rows, axis=0)
        stats_out[it] = tile
        stats_in[it, s] = tile

        def stat(i, target, sender):
            d = (s + i) % SPACE
            return pltpu.make_async_remote_copy(
                src_ref=stats_out.at[it],
                dst_ref=stats_in.at[it, s if sender else d],
                send_sem=st_send.at[it, d],
                recv_sem=st_recv.at[it, s if sender else d],
                device_id={"space": d},
                device_id_type=MESH,
            )

        def send(i, carry):
            stat(i, s, True).start()
            return carry

        def receive(i, carry):
            stat(i, s, False).wait_recv()
            return carry

        lax.fori_loop(1, SPACE, send, 0)
        lax.fori_loop(1, SPACE, receive, 0)
        every = stats_in[it]
        tops = every[:, 0:1, :]
        scale = jnp.exp(tops - jnp.max(tops, axis=0, keepdims=True))
        sums = jnp.sum(jnp.sum(every * scale, axis=0), axis=1, keepdims=True)
        return [sums[i : i + 1] / sums[1:2] for i in (2, 3, 4)]

    def make_ramp(shifts):
        by_z, by_x, by_y = shifts
        kz = lax.broadcasted_iota(jnp.int32, (Z, 128), 0)
        ky = lax.broadcasted_iota(jnp.int32, (Z, 128), 1)
        phase = (2.0 * math.pi) * (signed(kz, Z) * (by_z / Z) + signed(ky, Y) * (by_y / Y))
        ramp_zy[0] = jnp.cos(phase)
        ramp_zy[1] = jnp.sin(phase)
        kx = s * SLOTS + lax.broadcasted_iota(jnp.int32, (SLOTS, 128), 0)
        phase = (2.0 * math.pi) * (kx.astype(F32) * (by_x / X))
        cos_x, sin_x = jnp.cos(phase), jnp.sin(phase)
        for j in range(SLOTS):
            ramp_x[0, j] = jnp.broadcast_to(cos_x[j : j + 1], (8, 128))
            ramp_x[1, j] = jnp.broadcast_to(sin_x[j : j + 1], (8, 128))

    def shifted_slot(j):
        cos_x = jnp.concatenate([ramp_x[0, j]] * (Z // 8), axis=0)
        sin_x = jnp.concatenate([ramp_x[1, j]] * (Z // 8), axis=0)
        cosine = ramp_zy[0] * cos_x - ramp_zy[1] * sin_x
        sine = ramp_zy[1] * cos_x + ramp_zy[0] * sin_x
        f_re, f_im = slot_of(spec, j)
        return f_re * cosine - f_im * sine, f_re * sine + f_im * cosine

    def shifted_last():
        f_re, f_im = last_slot(spec)
        return f_re * ramp_zy[0] - f_im * ramp_zy[1], f_re * ramp_zy[1] + f_im * ramp_zy[0]

    for it in range(ITERS):
        if it > 0:

            def shift_one(j, carry):
                re, im = shifted_slot(j)
                moved[j, 0:Z, :] = re
                moved[j, Z : 2 * Z, :] = im
                return carry

            lax.fori_loop(0, SLOTS, shift_one, 0)
            value = jnp.concatenate(shifted_last(), axis=0)
            for u in range(SLOTS):
                moved[u, 2 * Z :, :] = value[8 * u : 8 * u + 8]
        template_sum(it, moved if it > 0 else spec)
        inverse(
            it,
            lambda j: whiten(*slot_of(spec, j), *slot_of(tmpl.at[it], j)),
            lambda: whiten(*last_slot(spec), *last_slot(tmpl.at[it])),
        )
        shifts = centroid(it)
        make_ramp(shifts)

    inverse(ITERS, shifted_slot, shifted_last)
    for z in range(0, SLABS, 2):
        value = cells(ITERS, z)
        for i in range(2):
            out_ref[z + i] = value[:, i * 128 : (i + 1) * 128]
    by_z, by_x, by_y = shifts
    line = jnp.where(lane == 0, by_z, jnp.where(lane == 1, by_x, by_y))
    shift_ref[...] = line[:, 0:3]

    for copy in sends:
        copy.wait_send()

    def finish(q, carry):
        wait_sent(send_f, recv_f, fwd_send, fwd_recv, q)
        for n in range(ITERS + 1):
            wait_sent(send_i.at[n], recv_i.at[n], inv_send.at[n], inv_recv.at[n], q)
        return carry

    lax.fori_loop(0, NQ, finish, 0)
    for it in range(ITERS):

        def done(i, carry):
            d = (s + i) % SPACE
            pltpu.make_async_remote_copy(
                src_ref=stats_out.at[it],
                dst_ref=stats_in.at[it, s],
                send_sem=st_send.at[it, d],
                recv_sem=st_recv.at[it, s],
                device_id={"space": d},
                device_id_type=MESH,
            ).wait_send()
            return carry

        lax.fori_loop(1, SPACE, done, 0)


def body(volumes):
    consts = [jnp.asarray(table) for table in tables()]
    vmem = pl.BlockSpec(memory_space=pltpu.VMEM)
    dma = pltpu.SemaphoreType.DMA
    corrected, shifts = pl.pallas_call(
        kernel,
        out_shape=(
            jax.ShapeDtypeStruct((SLABS, X, Y), F32),
            jax.ShapeDtypeStruct((1, 3), F32),
        ),
        in_specs=[vmem] * (1 + len(consts)),
        out_specs=(vmem, vmem),
        scratch_shapes=[
            pltpu.VMEM((ROWS, 128), F32),
            pltpu.VMEM((ROWS, 128), F32),
            pltpu.VMEM((SLOTS, UNIT, 128), F32),
            pltpu.VMEM((SLOTS, UNIT, 128), F32),
            pltpu.VMEM((ITERS, CHIPS, UNIT, 128), F32),
            pltpu.VMEM((ITERS, CHIPS, UNIT, 128), F32),
            pltpu.VMEM((ITERS, 4, UNIT, 128), F32),
            pltpu.VMEM((ITERS, 3, UNIT, 128), F32),
            pltpu.VMEM((ITERS, 4, UNIT, 128), F32),
            pltpu.VMEM((ITERS, 3, UNIT, 128), F32),
            pltpu.VMEM((ITERS, SLOTS, UNIT, 128), F32),
            pltpu.VMEM((ITERS + 1, ROWS, 128), F32),
            pltpu.VMEM((ITERS + 1, ROWS, 128), F32),
            pltpu.VMEM((SLABS, X, 128), F32),
            pltpu.VMEM((ITERS, 8, 128), F32),
            pltpu.VMEM((ITERS, SPACE, 8, 128), F32),
            pltpu.VMEM((2, Z, 128), F32),
            pltpu.VMEM((2, SLOTS, 8, 128), F32),
            dma((NQ, SPACE)), dma((NQ, SPACE)),
            dma((ITERS + 1, NQ, SPACE)), dma((ITERS + 1, NQ, SPACE)),
            dma((ITERS, SPACE)), dma((ITERS, SPACE)),
            dma((ITERS,)), dma((ITERS,)),
            dma((ITERS, 4)), dma((ITERS, 4)),
            dma((ITERS, 3)), dma((ITERS, 3)),
            dma((ITERS, 4)), dma((ITERS, 4)),
            dma((ITERS, 3)), dma((ITERS, 3)),
            dma((ITERS, CHIPS)), dma((ITERS, CHIPS)),
        ],
        compiler_params=pltpu.CompilerParams(
            collective_id=0, has_side_effects=True, vmem_limit_bytes=50 * 2**20
        ),
        name="register",
    )(volumes[0], *consts)
    return corrected[None], shifts


def solution(mesh):
    in_specs = (P("tm", "space", None, None),)
    out_specs = (P("tm", "space", None, None), P("tm", None))
    return jax.shard_map(body, mesh=mesh, in_specs=in_specs, out_specs=out_specs, check_vma=False)
```

```python
import functools
import math

import jax
import jax.numpy as jnp
import ml_dtypes
import numpy as np
from jax import lax
from jax.experimental import pallas as pl
from jax.experimental.pallas import tpu as pltpu
from jax.sharding import PartitionSpec as P

X = 512
Y = 128
Z = 64
ITERS = 2
FRAMES = 16
SHARPNESS = 256.0
FLOOR = 0.05 * (X * Y * Z)

SPACE = 16
CHIPS = 8
SLABS = Z // SPACE
SLOTS = X // 2 // SPACE
ROWS = SPACE * SLOTS * 8
MSG = SLOTS * 8
NQ = 4
PART = MSG // NQ
HALF = SLOTS // NQ * Z
UNIT = HALF // CHIPS
PAIRS = SLOTS // 2 // NQ
MESH = pl.DeviceIdType.MESH
F32 = jnp.float32
BF16 = jnp.bfloat16


def tables():
    def angles(n, rows, columns):
        return 2.0 * np.pi * ((rows[:, None] * columns[None, :]) % n) / n

    half = X // 2
    a = angles(X, np.arange(half), np.arange(X))
    sign = (-1.0) ** np.arange(X)
    cos_x, sin_x = np.cos(a), np.sin(a)
    im = -sin_x
    im[0] = sign
    forward_x = np.concatenate([cos_x, im])
    weight = np.full((X, 1), 2.0)
    weight[0] = weight[half] = 1.0
    inverse_x = (forward_x * weight).T / (X * Y * Z)

    a = angles(Y, np.arange(Y), np.arange(Y))
    c, s = np.cos(a), np.sin(a)
    forward_y = np.block([[c, -s], [s, c]])
    inverse_y = np.block([[c, s], [-s, c]])

    a = angles(Z, np.arange(Z), np.arange(Z))
    c, s = np.cos(a), np.sin(a)
    forward_z = np.block([[c, s], [-s, c]])
    inverse_z = np.block([[c, -s], [s, c]])
    order = np.arange(2 * Z).reshape(2, SPACE, SLABS).transpose(1, 0, 2).reshape(-1)
    forward_z = forward_z[:, order]
    inverse_z = inverse_z[order, :]

    out = []
    for table in (forward_x, inverse_x, forward_y, inverse_y, forward_z, inverse_z):
        high = table.astype(np.float32).astype(ml_dtypes.bfloat16)
        low = (table - high.astype(np.float64)).astype(np.float32).astype(ml_dtypes.bfloat16)
        out.append(np.stack([high, low]))
    flips = [np.zeros((n, n), ml_dtypes.bfloat16) for n in (Z, Y)]
    for flip in flips:
        flip[np.arange(len(flip)), -np.arange(len(flip))] = 1.0
    return out + flips


def split(value):
    high = value.astype(BF16)
    return high, (value - high.astype(F32)).astype(BF16)


def dot(a, b):
    return jnp.dot(a, b, preferred_element_type=F32)


def table_dot(table, data):
    data_high, data_low = split(data)
    return dot(table[0], data_high) + (dot(table[0], data_low) + dot(table[1], data_high))


def dot_table(data, table):
    data_high, data_low = split(data)
    return dot(data_high, table[0]) + (dot(data_low, table[0]) + dot(data_high, table[1]))


def rows_of(start, count):
    return pl.ds(pl.multiple_of(start, 8), count)


def signed(index, n):
    wrapped = jnp.where(index < n // 2, index, index - n)
    return jnp.where(index == n // 2, 0, wrapped).astype(F32)


def kernel(
    v_hbm, fx_hbm, ix_hbm, fy_hbm, iy_hbm, fz_hbm, iz_hbm, flip_z_hbm, flip_y_hbm,
    out_ref, shift_ref,
    v_ref, fx, ix, fy, iy, fz, iz, flip_z, flip_y,
    send_f, recv_f, spec, moved, first_f, last_f, first_t, last_t, other, pair,
    ring_r, ring_l, sent_r, sent_l, tmpl,
    send_i, recv_i, scores, stats_out, stats_in, ramp_zy, ramp_x,
    load_sem, fwd_send, fwd_recv, inv_send, inv_recv, st_send, st_recv,
    oc_send, oc_recv, rr_send, rr_recv, rl_send, rl_recv,
    gr_send, gr_recv, gl_send, gl_recv, go_send, go_recv,
):
    s = lax.axis_index("space")
    t = lax.axis_index("tm")
    core = t % 2
    chip = t // 2
    mate = chip * 2 + 1 - core
    right = ((chip + 1) % CHIPS) * 2 + core
    left = ((chip + CHIPS - 1) % CHIPS) * 2 + core

    loads = [
        pltpu.make_async_copy(source, target, load_sem.at[i])
        for i, (source, target) in enumerate(
            [
                (fx_hbm, fx), (v_hbm, v_ref), (fz_hbm, fz), (fy_hbm, fy), (iy_hbm, iy),
                (iz_hbm, iz), (flip_z_hbm, flip_z), (flip_y_hbm, flip_y), (ix_hbm, ix),
            ]
        )
    ]
    for copy in loads:
        copy.start()

    barrier = pltpu.get_barrier_semaphore()

    def greet(i, carry):
        pl.semaphore_signal(barrier, inc=1, device_id={"space": (s + i) % SPACE}, device_id_type=MESH)
        return carry

    lax.fori_loop(1, SPACE, greet, 0)
    for member in (mate, right, left):
        pl.semaphore_signal(barrier, inc=1, device_id={"tm": member}, device_id_type=MESH)

    row = lax.broadcasted_iota(jnp.int32, (2 * Z, 128), 0)
    first_part = (row // SLABS) % 2 == 0

    def to_space(source, start, target, target_start, send_sem, recv_sem, device, count):
        return pltpu.make_async_remote_copy(
            src_ref=source.at[rows_of(start, count)],
            dst_ref=target.at[rows_of(target_start, count)],
            send_sem=send_sem,
            recv_sem=recv_sem,
            device_id={"space": device},
            device_id_type=MESH,
        )

    for copy in loads[:2]:
        copy.wait()

    for z in range(0, SLABS, 2):
        data = jnp.concatenate([v_ref[z], v_ref[z + 1]], axis=1)
        result = table_dot(fx, data)
        for i in range(2):
            for part in range(2):
                send_f[pl.ds(part * SLABS + z + i, X // 2, stride=8), :] = result[
                    part * (X // 2) : (part + 1) * (X // 2), i * 128 : (i + 1) * 128
                ]

    pl.semaphore_wait(barrier, SPACE + 2)

    def exchange_part(source, target, send_sem, recv_sem, q):
        def one(i, carry):
            d = (s + i) % SPACE
            to_space(
                source, d * MSG + q * PART, target, s * MSG + q * PART,
                send_sem.at[q, d], recv_sem.at[q, s], d, PART,
            ).start()
            return carry

        lax.fori_loop(1, SPACE, one, 0)
        mine = rows_of(s * MSG + q * PART, PART)
        target[mine, :] = source[mine, :]

    def wait_part(source, target, send_sem, recv_sem, q):
        def one(i, carry):
            d = (s + i) % SPACE
            to_space(
                source, d * MSG + q * PART, target, d * MSG + q * PART,
                send_sem.at[q, d], recv_sem.at[q, d], d, PART,
            ).wait_recv()
            return carry

        lax.fori_loop(1, SPACE, one, 0)

    def wait_sent(source, target, send_sem, recv_sem, q):
        def one(i, carry):
            d = (s + i) % SPACE
            to_space(
                source, d * MSG + q * PART, target, s * MSG + q * PART,
                send_sem.at[q, d], recv_sem.at[q, s], d, PART,
            ).wait_send()
            return carry

        lax.fori_loop(1, SPACE, one, 0)

    def send_all(q, carry):
        exchange_part(send_f, recv_f, fwd_send, fwd_recv, q)
        return carry

    lax.fori_loop(0, NQ, send_all, 0)
    for copy in loads[2:]:
        copy.wait()

    def load_slot(j):
        return jnp.concatenate([recv_f[rows_of(d * MSG + j * 8, 8), :] for d in range(SPACE)], axis=0)

    def complex_rows(value):
        return jnp.concatenate([value[:Z], value[Z:]], axis=1)

    def part_rows(value):
        return jnp.concatenate([value[:, :128], value[:, 128:]], axis=0)

    def spectrum_two(a, b):
        zed = table_dot(fz, jnp.concatenate([a, b], axis=1))
        lines = jnp.concatenate([complex_rows(zed[:, :128]), complex_rows(zed[:, 128:])], axis=0)
        freq = dot_table(lines, fy)
        return part_rows(freq[:Z]), part_rows(freq[Z:])

    def slot_rows(j):
        return rows_of(j * 2 * Z, 2 * Z)

    def spectrum_pair(i, carry):
        j = 2 * i
        a, b = spectrum_two(load_slot(j), load_slot(j + 1))
        spec[slot_rows(j), :] = a
        spec[slot_rows(j + 1), :] = b
        return carry

    owner = jnp.where(s == 0, 1.0, 0.0)

    def forward_part(q):
        wait_part(send_f, recv_f, fwd_send, fwd_recv, q)
        lax.fori_loop(q * PAIRS, (q + 1) * PAIRS, spectrum_pair, 0)
        if q == 0:
            slot = load_slot(0)
            keep = jnp.where(first_part, 1.0, 1.0 - owner)
            rolled = jnp.concatenate([slot[SLABS:], slot[:SLABS]], axis=0)
            first_f[...], last_f[...] = spectrum_two(slot * keep, rolled * jnp.where(first_part, owner, 0.0))

    sends = []

    def to_tm(source, target, send_sem, recv_sem, device):
        return pltpu.make_async_remote_copy(
            src_ref=source,
            dst_ref=target,
            send_sem=send_sem,
            recv_sem=recv_sem,
            device_id={"tm": device},
            device_id_type=MESH,
        )

    def start(copy):
        copy.start()
        sends.append(copy)

    def half_rows(q, c):
        return rows_of((2 * q + c) * HALF, HALF)

    def sum_steps(it, q, source):
        def pair_unit(i):
            return pair.at[it, q, rows_of((i % CHIPS) * UNIT, UNIT)]

        def mean_unit(i):
            return tmpl.at[it, rows_of((2 * q + core) * HALF + (i % CHIPS) * UNIT, UNIT)]

        def swap():
            return to_tm(source.at[half_rows(q, 1 - core)], other.at[it, q], oc_send.at[it, q], oc_recv.at[it, q], mate)

        def sum_r(outgoing, k):
            return to_tm(outgoing, ring_r.at[it, q, k], rr_send.at[it, q, k], rr_recv.at[it, q, k], right)

        def sum_l(outgoing, k):
            return to_tm(outgoing, ring_l.at[it, q, k], rl_send.at[it, q, k], rl_recv.at[it, q, k], left)

        def mean_r(i, k):
            return to_tm(mean_unit(i), mean_unit(i), gr_send.at[it, q, k], gr_recv.at[it, q, k], right)

        def mean_l(i, k):
            return to_tm(mean_unit(i), mean_unit(i), gl_send.at[it, q, k], gl_recv.at[it, q, k], left)

        def to_mate(c):
            ref = tmpl.at[it, half_rows(q, c)]
            return to_tm(ref, ref, go_send.at[it, q], go_recv.at[it, q], mate)

        def step_swap():
            start(swap())

        def step_pair():
            swap().wait_recv()
            pair[it, q] = source[half_rows(q, core), :] + other[it, q]
            start(sum_r(pair_unit(chip + 4), 0))
            start(sum_l(pair_unit(chip + CHIPS - 3), 0))

        def step_sum(k):
            def run():
                sum_r(sent_r.at[it, q, k - 1], k - 1).wait_recv()
                sent_r[it, q, k - 1] = pair_unit(chip + 4 - k)[...] + ring_r[it, q, k - 1]
                start(sum_r(sent_r.at[it, q, k - 1], k))
                if k < 3:
                    sum_l(sent_l.at[it, q, k - 1], k - 1).wait_recv()
                    sent_l[it, q, k - 1] = pair_unit(chip + CHIPS - 3 + k)[...] + ring_l[it, q, k - 1]
                    start(sum_l(sent_l.at[it, q, k - 1], k))

            return run

        def step_mean():
            sum_l(ring_l.at[it, q, 2], 2).wait_recv()
            sum_r(ring_r.at[it, q, 3], 3).wait_recv()
            total = pair_unit(chip)[...] + (ring_r[it, q, 3] + ring_l[it, q, 2])
            tmpl[it, rows_of((2 * q + core) * HALF + chip * UNIT, UNIT), :] = total * (1.0 / FRAMES)
            start(mean_r(chip, 0))
            start(mean_l(chip, 0))

        def step_pass(k):
            def run():
                mean_r(chip + CHIPS - k, k - 1).wait_recv()
                start(mean_r(chip + CHIPS - k, k))
                if k < 3:
                    mean_l(chip + k, k - 1).wait_recv()
                    start(mean_l(chip + k, k))

            return run

        def step_share():
            mean_l(chip + 3, 2).wait_recv()
            mean_r(chip + 4, 3).wait_recv()
            start(to_mate(core))

        def step_end():
            to_mate(1 - core).wait_recv()

        return (
            [step_swap, step_pair]
            + [step_sum(k) for k in (1, 2, 3)]
            + [step_mean]
            + [step_pass(k) for k in (1, 2, 3)]
            + [step_share, step_end]
        )

    def whiten(f_re, f_im, t_re, t_im):
        p_re = f_re * t_re + f_im * t_im
        p_im = f_im * t_re - f_re * t_im
        scale = lax.rsqrt(jnp.maximum(p_re * p_re + p_im * p_im, FLOOR * FLOOR))
        return p_re * scale, p_im * scale

    def halves(value):
        return value[:Z], value[Z:]

    def slot_of(ref, first, j):
        return halves(jnp.where(j == 0, first[...], ref[slot_rows(j), :]))

    def packed(first, last):
        (f_re, f_im), (l_re, l_im) = first, last
        return jnp.concatenate([f_re - l_im, f_im + l_re], axis=0)

    def flipped(value):
        high, low = split(value)
        value = dot(flip_z[...], high) + dot(flip_z[...], low)
        high, low = split(part_rows(value))
        return halves(dot(high, flip_y[...]) + dot(low, flip_y[...]))

    def unpack(it):
        value = tmpl[it, slot_rows(0), :]
        re, im = halves(value)
        flip_re, flip_im = flipped(complex_rows(value))
        half = 0.5 * owner
        first_t[it] = jnp.concatenate([re - half * (re - flip_re), im - half * (im + flip_im)], axis=0)
        last_t[it] = jnp.concatenate([half * (im + flip_im), half * (flip_re - re)], axis=0)

    def back(values):
        lines = [jnp.concatenate([re, im], axis=1) for re, im in values]
        lines = dot_table(jnp.concatenate(lines, axis=0), iy)
        planes = [part_rows(lines[i * Z : (i + 1) * Z]) for i in range(len(values))]
        return table_dot(iz, jnp.concatenate(planes, axis=1))

    def inverse_part(n, q, slot_values, last_values):
        if q == 0:
            last = back([last_values()])
            last = jnp.concatenate([last[2 * Z - SLABS :], last[: 2 * Z - SLABS]], axis=0)

        def pair_back(i, carry):
            j = 2 * i
            planes = back([slot_values(j), slot_values(j + 1)])
            values = [planes[:, :128], planes[:, 128:]]
            if q == 0:
                keep = jnp.where(first_part, 1.0, jnp.where(s + j == 0, 0.0, 1.0))
                values[0] = values[0] * keep + last * (1.0 - keep)
            for k in range(2):
                for d in range(SPACE):
                    send_i[n, rows_of(d * MSG + (j + k) * 8, 8), :] = values[k][8 * d : 8 * d + 8]
            return carry

        lax.fori_loop(q * PAIRS, (q + 1) * PAIRS, pair_back, 0)
        exchange_part(send_i.at[n], recv_i.at[n], inv_send.at[n], inv_recv.at[n], q)

    def inverse_wait(n):
        def one(q, carry):
            wait_part(send_i.at[n], recv_i.at[n], inv_send.at[n], inv_recv.at[n], q)
            return carry

        lax.fori_loop(0, NQ, one, 0)

    def cells(n, z):
        columns = []
        for i in range(2):
            parts = [
                recv_i[n, pl.ds(part * SLABS + z + i, X // 2, stride=8), :] for part in range(2)
            ]
            columns.append(jnp.concatenate(parts, axis=0))
        return table_dot(ix, jnp.concatenate(columns, axis=1))

    lane = lax.broadcasted_iota(jnp.int32, (1, 128), 1)

    def centroid(it):
        top = jnp.full((8, 128), -jnp.inf, F32)
        for z in range(0, SLABS, 2):
            value = cells(it, z) * SHARPNESS
            for i in range(2):
                plane = value[:, i * 128 : (i + 1) * 128]
                scores[z + i] = plane
                top = jnp.maximum(top, jnp.max(plane.reshape(X // 8, 8, 128), axis=0))
        top = jnp.max(jnp.max(top, axis=0, keepdims=True), axis=1, keepdims=True)
        step = 128
        x_row = lax.broadcasted_iota(jnp.int32, (step, 128), 0)
        zero = jnp.zeros((8, 128), F32)

        def weigh(i, carry):
            total, by_z, by_x = carry
            z, x = i // (X // step), (i % (X // step)) * step
            weights = jnp.exp(scores[z, rows_of(x, step), :] - top)
            x_at = ((x + x_row + X // 2) % X - X // 2).astype(F32)
            z_at = ((s * SLABS + z + Z // 2) % Z - Z // 2).astype(F32)
            here = jnp.sum(weights.reshape(step // 8, 8, 128), axis=0)
            by_x = by_x + jnp.sum((weights * x_at).reshape(step // 8, 8, 128), axis=0)
            return total + here, by_z + here * z_at, by_x

        total, by_z, by_x = lax.fori_loop(0, SLABS * X // step, weigh, (zero, zero, zero))
        y_at = ((lane + Y // 2) % Y - Y // 2).astype(F32)
        sums = [jnp.sum(value, axis=0, keepdims=True) for value in (total, by_z, by_x)]
        rows = [jnp.broadcast_to(top, (1, 128))] + sums + [sums[0] * y_at, jnp.zeros((3, 128), F32)]
        tile = jnp.concatenate(rows, axis=0)
        stats_out[it] = tile
        stats_in[it, s] = tile

        def stat(i, target, sender):
            d = (s + i) % SPACE
            return pltpu.make_async_remote_copy(
                src_ref=stats_out.at[it],
                dst_ref=stats_in.at[it, s if sender else d],
                send_sem=st_send.at[it, d],
                recv_sem=st_recv.at[it, s if sender else d],
                device_id={"space": d},
                device_id_type=MESH,
            )

        def send(i, carry):
            stat(i, s, True).start()
            return carry

        def receive(i, carry):
            stat(i, s, False).wait_recv()
            return carry

        lax.fori_loop(1, SPACE, send, 0)
        lax.fori_loop(1, SPACE, receive, 0)
        every = stats_in[it]
        tops = every[:, 0:1, :]
        scale = jnp.exp(tops - jnp.max(tops, axis=0, keepdims=True))
        sums = jnp.sum(jnp.sum(every * scale, axis=0), axis=1, keepdims=True)
        return [sums[i : i + 1] / sums[1:2] for i in (2, 3, 4)]

    def make_ramp(shifts):
        by_z, by_x, by_y = shifts
        kz = lax.broadcasted_iota(jnp.int32, (Z, 128), 0)
        ky = lax.broadcasted_iota(jnp.int32, (Z, 128), 1)
        phase = (2.0 * math.pi) * (signed(kz, Z) * (by_z / Z) + signed(ky, Y) * (by_y / Y))
        ramp_zy[0] = jnp.cos(phase)
        ramp_zy[1] = jnp.sin(phase)
        kx = s * SLOTS + lax.broadcasted_iota(jnp.int32, (SLOTS, 128), 0)
        phase = (2.0 * math.pi) * (kx.astype(F32) * (by_x / X))
        cos_x, sin_x = jnp.cos(phase), jnp.sin(phase)
        for j in range(SLOTS):
            ramp_x[0, j] = jnp.broadcast_to(cos_x[j : j + 1], (8, 128))
            ramp_x[1, j] = jnp.broadcast_to(sin_x[j : j + 1], (8, 128))

    def shifted_slot(j):
        cos_x = jnp.concatenate([ramp_x[0, j]] * (Z // 8), axis=0)
        sin_x = jnp.concatenate([ramp_x[1, j]] * (Z // 8), axis=0)
        cosine = ramp_zy[0] * cos_x - ramp_zy[1] * sin_x
        sine = ramp_zy[1] * cos_x + ramp_zy[0] * sin_x
        f_re, f_im = slot_of(spec, first_f, j)
        return f_re * cosine - f_im * sine, f_re * sine + f_im * cosine

    def shifted_last():
        f_re, f_im = halves(last_f[...])
        return f_re * ramp_zy[0] - f_im * ramp_zy[1], f_re * ramp_zy[1] + f_im * ramp_zy[0]

    def shift_one(j, carry):
        moved[slot_rows(j), :] = jnp.concatenate(shifted_slot(j), axis=0)
        return carry

    def shift_part(q):
        lax.fori_loop(q * 2 * PAIRS, (q + 1) * 2 * PAIRS, shift_one, 0)
        if q == 0:
            moved[slot_rows(0), :] = packed(halves(moved[slot_rows(0), :]), shifted_last())

    for it in range(ITERS):

        def part_steps(q):
            def begin():
                if it == 0:
                    forward_part(q)
                else:
                    shift_part(q)

            def end():
                if q == 0:
                    unpack(it)
                inverse_part(
                    it,
                    q,
                    lambda j: whiten(*slot_of(spec, first_f, j), *slot_of(tmpl.at[it], first_t.at[it], j)),
                    lambda: whiten(*halves(last_f[...]), *halves(last_t[it])),
                )

            steps = sum_steps(it, q, moved if it > 0 else spec)
            return [lambda: (begin(), steps[0]())] + steps[1:-1] + [lambda: (steps[-1](), end())]

        plan = [part_steps(q) for q in range(NQ)]
        for wave in range(NQ + len(plan[0]) - 1):
            for q in range(NQ):
                if 0 <= wave - q < len(plan[q]):
                    plan[q][wave - q]()
        inverse_wait(it)
        shifts = centroid(it)
        make_ramp(shifts)

    for q in range(NQ):
        inverse_part(ITERS, q, shifted_slot, shifted_last)
    inverse_wait(ITERS)
    for z in range(0, SLABS, 2):
        value = cells(ITERS, z)
        for i in range(2):
            out_ref[z + i] = value[:, i * 128 : (i + 1) * 128]
    by_z, by_x, by_y = shifts
    line = jnp.where(lane == 0, by_z, jnp.where(lane == 1, by_x, by_y))
    shift_ref[...] = line[:, 0:3]

    for copy in sends:
        copy.wait_send()

    def finish(q, carry):
        wait_sent(send_f, recv_f, fwd_send, fwd_recv, q)
        for n in range(ITERS + 1):
            wait_sent(send_i.at[n], recv_i.at[n], inv_send.at[n], inv_recv.at[n], q)
        return carry

    lax.fori_loop(0, NQ, finish, 0)
    for it in range(ITERS):

        def done(i, carry):
            d = (s + i) % SPACE
            pltpu.make_async_remote_copy(
                src_ref=stats_out.at[it],
                dst_ref=stats_in.at[it, s],
                send_sem=st_send.at[it, d],
                recv_sem=st_recv.at[it, s],
                device_id={"space": d},
                device_id_type=MESH,
            ).wait_send()
            return carry

        lax.fori_loop(1, SPACE, done, 0)


def body(volumes):
    consts = [jnp.asarray(table) for table in tables()]
    vmem = pl.BlockSpec(memory_space=pltpu.VMEM)
    hbm = pl.BlockSpec(memory_space=pltpu.HBM)
    dma = pltpu.SemaphoreType.DMA
    slots = SLOTS * 2 * Z
    corrected, shifts = pl.pallas_call(
        kernel,
        out_shape=(
            jax.ShapeDtypeStruct((SLABS, X, Y), F32),
            jax.ShapeDtypeStruct((1, 3), F32),
        ),
        in_specs=[hbm] * (1 + len(consts)),
        out_specs=(vmem, vmem),
        scratch_shapes=[
            pltpu.VMEM((SLABS, X, Y), F32),
            *[pltpu.VMEM(table.shape, BF16) for table in consts],
            pltpu.VMEM((ROWS, 128), F32),
            pltpu.VMEM((ROWS, 128), F32),
            pltpu.VMEM((slots, 128), F32),
            pltpu.VMEM((slots, 128), F32),
            pltpu.VMEM((2 * Z, 128), F32),
            pltpu.VMEM((2 * Z, 128), F32),
            pltpu.VMEM((ITERS, 2 * Z, 128), F32),
            pltpu.VMEM((ITERS, 2 * Z, 128), F32),
            pltpu.VMEM((ITERS, NQ, HALF, 128), F32),
            pltpu.VMEM((ITERS, NQ, HALF, 128), F32),
            pltpu.VMEM((ITERS, NQ, 4, UNIT, 128), F32),
            pltpu.VMEM((ITERS, NQ, 3, UNIT, 128), F32),
            pltpu.VMEM((ITERS, NQ, 3, UNIT, 128), F32),
            pltpu.VMEM((ITERS, NQ, 2, UNIT, 128), F32),
            pltpu.VMEM((ITERS, slots, 128), F32),
            pltpu.VMEM((ITERS + 1, ROWS, 128), F32),
            pltpu.VMEM((ITERS + 1, ROWS, 128), F32),
            pltpu.VMEM((SLABS, X, 128), F32),
            pltpu.VMEM((ITERS, 8, 128), F32),
            pltpu.VMEM((ITERS, SPACE, 8, 128), F32),
            pltpu.VMEM((2, Z, 128), F32),
            pltpu.VMEM((2, SLOTS, 8, 128), F32),
            dma((1 + len(consts),)),
            dma((NQ, SPACE)), dma((NQ, SPACE)),
            dma((ITERS + 1, NQ, SPACE)), dma((ITERS + 1, NQ, SPACE)),
            dma((ITERS, SPACE)), dma((ITERS, SPACE)),
            dma((ITERS, NQ)), dma((ITERS, NQ)),
            dma((ITERS, NQ, 4)), dma((ITERS, NQ, 4)),
            dma((ITERS, NQ, 3)), dma((ITERS, NQ, 3)),
            dma((ITERS, NQ, 4)), dma((ITERS, NQ, 4)),
            dma((ITERS, NQ, 3)), dma((ITERS, NQ, 3)),
            dma((ITERS, NQ)), dma((ITERS, NQ)),
        ],
        compiler_params=pltpu.CompilerParams(
            collective_id=0, has_side_effects=True, vmem_limit_bytes=56 * 2**20
        ),
        name="register",
    )(volumes[0], *consts)
    return corrected[None], shifts


def solution(mesh):
    in_specs = (P("tm", "space", None, None),)
    out_specs = (P("tm", "space", None, None), P("tm", None))
    return jax.shard_map(body, mesh=mesh, in_specs=in_specs, out_specs=out_specs, check_vma=False)
```

```python
import functools
import math

import jax
import jax.numpy as jnp
import ml_dtypes
import numpy as np
from jax import lax
from jax.experimental import pallas as pl
from jax.experimental.pallas import tpu as pltpu
from jax.sharding import PartitionSpec as P

X = 512
Y = 128
Z = 64
ITERS = 2
FRAMES = 16
SHARPNESS = 256.0
FLOOR = 0.05 * (X * Y * Z)

SPACE = 16
CHIPS = 8
SLABS = Z // SPACE
SLOTS = X // 2 // SPACE
ROWS = SPACE * SLOTS * 8
MSG = SLOTS * 8
NQ = 4
PART = MSG // NQ
HALF = SLOTS // NQ * Z
UNIT = HALF // CHIPS
PAIRS = SLOTS // 2 // NQ
FIRST_SUMS = ((2, 1), (4, 1), (-3, -1), (-1, -1))
MERGED = (1, 3, -2)
MEANS = (-1, -3, 2, 1)
PASSED = ((1, -1), (3, -1), (-2, 1))
LAST_MEANS = (-1, 2, 4, -3)
REACHED = (1, -1, 2, -2, 3, -3)
MESH = pl.DeviceIdType.MESH
F32 = jnp.float32
BF16 = jnp.bfloat16


def tables():
    def angles(n, rows, columns):
        return 2.0 * np.pi * ((rows[:, None] * columns[None, :]) % n) / n

    half = X // 2
    a = angles(X, np.arange(half), np.arange(X))
    sign = (-1.0) ** np.arange(X)
    cos_x, sin_x = np.cos(a), np.sin(a)
    im = -sin_x
    im[0] = sign
    forward_x = np.concatenate([cos_x, im])
    weight = np.full((X, 1), 2.0)
    weight[0] = weight[half] = 1.0
    inverse_x = (forward_x * weight).T / (X * Y * Z)

    a = angles(Y, np.arange(Y), np.arange(Y))
    c, s = np.cos(a), np.sin(a)
    forward_y = np.block([[c, -s], [s, c]])
    inverse_y = np.block([[c, s], [-s, c]])

    a = angles(Z, np.arange(Z), np.arange(Z))
    c, s = np.cos(a), np.sin(a)
    forward_z = np.block([[c, s], [-s, c]])
    inverse_z = np.block([[c, -s], [s, c]])
    order = np.arange(2 * Z).reshape(2, SPACE, SLABS).transpose(1, 0, 2).reshape(-1)
    forward_z = forward_z[:, order]
    inverse_z = inverse_z[order, :]

    out = []
    for table in (forward_x, inverse_x, forward_y, inverse_y, forward_z, inverse_z):
        high = table.astype(np.float32).astype(ml_dtypes.bfloat16)
        low = (table - high.astype(np.float64)).astype(np.float32).astype(ml_dtypes.bfloat16)
        out.append(np.stack([high, low]))
    flips = [np.zeros((n, n), ml_dtypes.bfloat16) for n in (Z, Y)]
    for flip in flips:
        flip[np.arange(len(flip)), -np.arange(len(flip))] = 1.0
    return out + flips


def split(value):
    high = value.astype(BF16)
    return high, (value - high.astype(F32)).astype(BF16)


def dot(a, b):
    return jnp.dot(a, b, preferred_element_type=F32)


def table_dot(table, data):
    data_high, data_low = split(data)
    return dot(table[0], data_high) + (dot(table[0], data_low) + dot(table[1], data_high))


def dot_table(data, table):
    data_high, data_low = split(data)
    return dot(data_high, table[0]) + (dot(data_low, table[0]) + dot(data_high, table[1]))


def rows_of(start, count):
    return pl.ds(pl.multiple_of(start, 8), count)


def signed(index, n):
    wrapped = jnp.where(index < n // 2, index, index - n)
    return jnp.where(index == n // 2, 0, wrapped).astype(F32)


def kernel(
    v_hbm, fx_hbm, ix_hbm, fy_hbm, iy_hbm, fz_hbm, iz_hbm, flip_z_hbm, flip_y_hbm,
    out_ref, shift_ref,
    v_ref, fx, ix, fy, iy, fz, iz, flip_z, flip_y,
    send_f, recv_f, spec, moved, first_f, last_f, first_t, last_t, other, pair,
    sums_in, sums_out, tmpl,
    send_i, recv_i, scores, stats_out, stats_in, ramp_zy, ramp_x,
    load_sem, fwd_send, fwd_recv, inv_send, inv_recv, st_send, st_recv,
    oc_send, oc_recv, sum_send, sum_recv, mean_send, mean_recv, go_send, go_recv,
):
    s = lax.axis_index("space")
    t = lax.axis_index("tm")
    core = t % 2
    chip = t // 2
    mate = chip * 2 + 1 - core

    loads = [
        pltpu.make_async_copy(source, target, load_sem.at[i])
        for i, (source, target) in enumerate(
            [
                (fx_hbm, fx), (v_hbm, v_ref), (fz_hbm, fz), (fy_hbm, fy), (iy_hbm, iy),
                (iz_hbm, iz), (flip_z_hbm, flip_z), (flip_y_hbm, flip_y), (ix_hbm, ix),
            ]
        )
    ]
    for copy in loads:
        copy.start()

    barrier = pltpu.get_barrier_semaphore()

    def greet(i, carry):
        pl.semaphore_signal(barrier, inc=1, device_id={"space": (s + i) % SPACE}, device_id_type=MESH)
        return carry

    lax.fori_loop(1, SPACE, greet, 0)
    for offset in REACHED:
        member = ((chip + CHIPS + offset) % CHIPS) * 2 + core
        pl.semaphore_signal(barrier, inc=1, device_id={"tm": member}, device_id_type=MESH)
    pl.semaphore_signal(barrier, inc=1, device_id={"tm": mate}, device_id_type=MESH)

    row = lax.broadcasted_iota(jnp.int32, (2 * Z, 128), 0)
    first_part = (row // SLABS) % 2 == 0

    def to_space(source, start, target, target_start, send_sem, recv_sem, device, count):
        return pltpu.make_async_remote_copy(
            src_ref=source.at[rows_of(start, count)],
            dst_ref=target.at[rows_of(target_start, count)],
            send_sem=send_sem,
            recv_sem=recv_sem,
            device_id={"space": device},
            device_id_type=MESH,
        )

    for copy in loads[:2]:
        copy.wait()

    for z in range(0, SLABS, 2):
        data = jnp.concatenate([v_ref[z], v_ref[z + 1]], axis=1)
        result = table_dot(fx, data)
        for i in range(2):
            for part in range(2):
                send_f[pl.ds(part * SLABS + z + i, X // 2, stride=8), :] = result[
                    part * (X // 2) : (part + 1) * (X // 2), i * 128 : (i + 1) * 128
                ]

    pl.semaphore_wait(barrier, SPACE + len(REACHED))

    def exchange_part(source, target, send_sem, recv_sem, q):
        def one(i, carry):
            d = (s + i) % SPACE
            to_space(
                source, d * MSG + q * PART, target, s * MSG + q * PART,
                send_sem.at[q, d], recv_sem.at[q, s], d, PART,
            ).start()
            return carry

        lax.fori_loop(1, SPACE, one, 0)
        mine = rows_of(s * MSG + q * PART, PART)
        target[mine, :] = source[mine, :]

    def wait_part(source, target, send_sem, recv_sem, q):
        def one(i, carry):
            d = (s + i) % SPACE
            to_space(
                source, d * MSG + q * PART, target, d * MSG + q * PART,
                send_sem.at[q, d], recv_sem.at[q, d], d, PART,
            ).wait_recv()
            return carry

        lax.fori_loop(1, SPACE, one, 0)

    def wait_sent(source, target, send_sem, recv_sem, q):
        def one(i, carry):
            d = (s + i) % SPACE
            to_space(
                source, d * MSG + q * PART, target, s * MSG + q * PART,
                send_sem.at[q, d], recv_sem.at[q, s], d, PART,
            ).wait_send()
            return carry

        lax.fori_loop(1, SPACE, one, 0)

    def send_all(q, carry):
        exchange_part(send_f, recv_f, fwd_send, fwd_recv, q)
        return carry

    lax.fori_loop(0, NQ, send_all, 0)
    for copy in loads[2:]:
        copy.wait()

    def load_slot(j):
        return jnp.concatenate([recv_f[rows_of(d * MSG + j * 8, 8), :] for d in range(SPACE)], axis=0)

    def complex_rows(value):
        return jnp.concatenate([value[:Z], value[Z:]], axis=1)

    def part_rows(value):
        return jnp.concatenate([value[:, :128], value[:, 128:]], axis=0)

    def spectrum_two(a, b):
        zed = table_dot(fz, jnp.concatenate([a, b], axis=1))
        lines = jnp.concatenate([complex_rows(zed[:, :128]), complex_rows(zed[:, 128:])], axis=0)
        freq = dot_table(lines, fy)
        return part_rows(freq[:Z]), part_rows(freq[Z:])

    def slot_rows(j):
        return rows_of(j * 2 * Z, 2 * Z)

    def spectrum_pair(i, carry):
        j = 2 * i
        a, b = spectrum_two(load_slot(j), load_slot(j + 1))
        spec[slot_rows(j), :] = a
        spec[slot_rows(j + 1), :] = b
        return carry

    owner = jnp.where(s == 0, 1.0, 0.0)

    def forward_part(q):
        wait_part(send_f, recv_f, fwd_send, fwd_recv, q)
        lax.fori_loop(q * PAIRS, (q + 1) * PAIRS, spectrum_pair, 0)
        if q == 0:
            slot = load_slot(0)
            keep = jnp.where(first_part, 1.0, 1.0 - owner)
            rolled = jnp.concatenate([slot[SLABS:], slot[:SLABS]], axis=0)
            first_f[...], last_f[...] = spectrum_two(slot * keep, rolled * jnp.where(first_part, owner, 0.0))

    sends = []

    def to_tm(source, target, send_sem, recv_sem, device):
        return pltpu.make_async_remote_copy(
            src_ref=source,
            dst_ref=target,
            send_sem=send_sem,
            recv_sem=recv_sem,
            device_id={"tm": device},
            device_id_type=MESH,
        )

    def start(copy):
        copy.start()
        sends.append(copy)

    def half_rows(q, c):
        return rows_of((2 * q + c) * HALF, HALF)

    def sum_steps(it, q, source):
        def pair_unit(i):
            return pair.at[it, q, rows_of((i % CHIPS) * UNIT, UNIT)]

        def mean_unit(i):
            return tmpl.at[it, rows_of((2 * q + core) * HALF + (i % CHIPS) * UNIT, UNIT)]

        def swap():
            return to_tm(source.at[half_rows(q, 1 - core)], other.at[it, q], oc_send.at[it, q], oc_recv.at[it, q], mate)

        def chip_at(offset):
            return ((chip + CHIPS + offset) % CHIPS) * 2 + core

        def sum_copy(outgoing, k, offset):
            return to_tm(outgoing, sums_in.at[it, q, k], sum_send.at[it, q, k], sum_recv.at[it, q, k], chip_at(offset))

        def mean_copy(i, k, offset):
            ref = mean_unit(chip + CHIPS + i)
            return to_tm(ref, ref, mean_send.at[it, q, k], mean_recv.at[it, q, k], chip_at(offset))

        def to_mate(c):
            ref = tmpl.at[it, half_rows(q, c)]
            return to_tm(ref, ref, go_send.at[it, q], go_recv.at[it, q], mate)

        def step_swap():
            start(swap())

        def step_pair():
            swap().wait_recv()
            pair[it, q] = source[half_rows(q, core), :] + other[it, q]
            for k, (i, offset) in enumerate(FIRST_SUMS):
                start(sum_copy(pair_unit(chip + CHIPS + i), k, offset))

        def step_merge():
            for k, i in enumerate(MERGED):
                sum_copy(sums_out.at[it, q, k], k, i).wait_recv()
                sums_out[it, q, k] = pair_unit(chip + CHIPS + i)[...] + sums_in[it, q, k]
                start(sum_copy(sums_out.at[it, q, k], 4 + k, i))

        def step_mean():
            total = pair_unit(chip)[...]
            for k in range(3, 7):
                sum_copy(sums_in.at[it, q, k], k, 1).wait_recv()
                total = total + sums_in[it, q, k]
            tmpl[it, rows_of((2 * q + core) * HALF + chip * UNIT, UNIT), :] = total * (1.0 / FRAMES)
            for k, offset in enumerate(MEANS):
                start(mean_copy(0, k, offset))

        def step_pass():
            for k, (i, offset) in enumerate(PASSED):
                mean_copy(i, k, 1).wait_recv()
                start(mean_copy(i, 4 + k, offset))

        def step_share():
            for k, i in enumerate(LAST_MEANS):
                mean_copy(i, 3 + k, 1).wait_recv()
            start(to_mate(core))

        def step_end():
            to_mate(1 - core).wait_recv()

        return [step_swap, step_pair, step_merge, step_mean, step_pass, step_share, step_end]

    def whiten(f_re, f_im, t_re, t_im):
        p_re = f_re * t_re + f_im * t_im
        p_im = f_im * t_re - f_re * t_im
        scale = lax.rsqrt(jnp.maximum(p_re * p_re + p_im * p_im, FLOOR * FLOOR))
        return p_re * scale, p_im * scale

    def halves(value):
        return value[:Z], value[Z:]

    def slot_of(ref, first, j):
        return halves(jnp.where(j == 0, first[...], ref[slot_rows(j), :]))

    def packed(first, last):
        (f_re, f_im), (l_re, l_im) = first, last
        return jnp.concatenate([f_re - l_im, f_im + l_re], axis=0)

    def flipped(value):
        high, low = split(value)
        value = dot(flip_z[...], high) + dot(flip_z[...], low)
        high, low = split(part_rows(value))
        return halves(dot(high, flip_y[...]) + dot(low, flip_y[...]))

    def unpack(it):
        value = tmpl[it, slot_rows(0), :]
        re, im = halves(value)
        flip_re, flip_im = flipped(complex_rows(value))
        half = 0.5 * owner
        first_t[it] = jnp.concatenate([re - half * (re - flip_re), im - half * (im + flip_im)], axis=0)
        last_t[it] = jnp.concatenate([half * (im + flip_im), half * (flip_re - re)], axis=0)

    def back(values):
        lines = [jnp.concatenate([re, im], axis=1) for re, im in values]
        lines = dot_table(jnp.concatenate(lines, axis=0), iy)
        planes = [part_rows(lines[i * Z : (i + 1) * Z]) for i in range(len(values))]
        return table_dot(iz, jnp.concatenate(planes, axis=1))

    def inverse_part(n, q, slot_values, last_values):
        if q == 0:
            last = back([last_values()])
            last = jnp.concatenate([last[2 * Z - SLABS :], last[: 2 * Z - SLABS]], axis=0)

        def pair_back(i, carry):
            j = 2 * i
            planes = back([slot_values(j), slot_values(j + 1)])
            values = [planes[:, :128], planes[:, 128:]]
            if q == 0:
                keep = jnp.where(first_part, 1.0, jnp.where(s + j == 0, 0.0, 1.0))
                values[0] = values[0] * keep + last * (1.0 - keep)
            for k in range(2):
                for d in range(SPACE):
                    send_i[n, rows_of(d * MSG + (j + k) * 8, 8), :] = values[k][8 * d : 8 * d + 8]
            return carry

        lax.fori_loop(q * PAIRS, (q + 1) * PAIRS, pair_back, 0)
        exchange_part(send_i.at[n], recv_i.at[n], inv_send.at[n], inv_recv.at[n], q)

    def inverse_wait(n):
        def one(q, carry):
            wait_part(send_i.at[n], recv_i.at[n], inv_send.at[n], inv_recv.at[n], q)
            return carry

        lax.fori_loop(0, NQ, one, 0)

    def cells(n, z):
        columns = []
        for i in range(2):
            parts = [
                recv_i[n, pl.ds(part * SLABS + z + i, X // 2, stride=8), :] for part in range(2)
            ]
            columns.append(jnp.concatenate(parts, axis=0))
        return table_dot(ix, jnp.concatenate(columns, axis=1))

    lane = lax.broadcasted_iota(jnp.int32, (1, 128), 1)

    def centroid(it):
        top = jnp.full((8, 128), -jnp.inf, F32)
        for z in range(0, SLABS, 2):
            value = cells(it, z) * SHARPNESS
            for i in range(2):
                plane = value[:, i * 128 : (i + 1) * 128]
                scores[z + i] = plane
                top = jnp.maximum(top, jnp.max(plane.reshape(X // 8, 8, 128), axis=0))
        top = jnp.max(jnp.max(top, axis=0, keepdims=True), axis=1, keepdims=True)
        step = 128
        x_row = lax.broadcasted_iota(jnp.int32, (step, 128), 0)
        zero = jnp.zeros((8, 128), F32)

        def weigh(i, carry):
            total, by_z, by_x = carry
            z, x = i // (X // step), (i % (X // step)) * step
            weights = jnp.exp(scores[z, rows_of(x, step), :] - top)
            x_at = ((x + x_row + X // 2) % X - X // 2).astype(F32)
            z_at = ((s * SLABS + z + Z // 2) % Z - Z // 2).astype(F32)
            here = jnp.sum(weights.reshape(step // 8, 8, 128), axis=0)
            by_x = by_x + jnp.sum((weights * x_at).reshape(step // 8, 8, 128), axis=0)
            return total + here, by_z + here * z_at, by_x

        total, by_z, by_x = lax.fori_loop(0, SLABS * X // step, weigh, (zero, zero, zero))
        y_at = ((lane + Y // 2) % Y - Y // 2).astype(F32)
        sums = [jnp.sum(value, axis=0, keepdims=True) for value in (total, by_z, by_x)]
        rows = [jnp.broadcast_to(top, (1, 128))] + sums + [sums[0] * y_at, jnp.zeros((3, 128), F32)]
        tile = jnp.concatenate(rows, axis=0)
        stats_out[it] = tile
        stats_in[it, s] = tile

        def stat(i, target, sender):
            d = (s + i) % SPACE
            return pltpu.make_async_remote_copy(
                src_ref=stats_out.at[it],
                dst_ref=stats_in.at[it, s if sender else d],
                send_sem=st_send.at[it, d],
                recv_sem=st_recv.at[it, s if sender else d],
                device_id={"space": d},
                device_id_type=MESH,
            )

        def send(i, carry):
            stat(i, s, True).start()
            return carry

        def receive(i, carry):
            stat(i, s, False).wait_recv()
            return carry

        lax.fori_loop(1, SPACE, send, 0)
        lax.fori_loop(1, SPACE, receive, 0)
        every = stats_in[it]
        tops = every[:, 0:1, :]
        scale = jnp.exp(tops - jnp.max(tops, axis=0, keepdims=True))
        sums = jnp.sum(jnp.sum(every * scale, axis=0), axis=1, keepdims=True)
        return [sums[i : i + 1] / sums[1:2] for i in (2, 3, 4)]

    def make_ramp(shifts):
        by_z, by_x, by_y = shifts
        kz = lax.broadcasted_iota(jnp.int32, (Z, 128), 0)
        ky = lax.broadcasted_iota(jnp.int32, (Z, 128), 1)
        phase = (2.0 * math.pi) * (signed(kz, Z) * (by_z / Z) + signed(ky, Y) * (by_y / Y))
        ramp_zy[0] = jnp.cos(phase)
        ramp_zy[1] = jnp.sin(phase)
        kx = s * SLOTS + lax.broadcasted_iota(jnp.int32, (SLOTS, 128), 0)
        phase = (2.0 * math.pi) * (kx.astype(F32) * (by_x / X))
        cos_x, sin_x = jnp.cos(phase), jnp.sin(phase)
        for j in range(SLOTS):
            ramp_x[0, j] = jnp.broadcast_to(cos_x[j : j + 1], (8, 128))
            ramp_x[1, j] = jnp.broadcast_to(sin_x[j : j + 1], (8, 128))

    def shifted_slot(j):
        cos_x = jnp.concatenate([ramp_x[0, j]] * (Z // 8), axis=0)
        sin_x = jnp.concatenate([ramp_x[1, j]] * (Z // 8), axis=0)
        cosine = ramp_zy[0] * cos_x - ramp_zy[1] * sin_x
        sine = ramp_zy[1] * cos_x + ramp_zy[0] * sin_x
        f_re, f_im = slot_of(spec, first_f, j)
        return f_re * cosine - f_im * sine, f_re * sine + f_im * cosine

    def shifted_last():
        f_re, f_im = halves(last_f[...])
        return f_re * ramp_zy[0] - f_im * ramp_zy[1], f_re * ramp_zy[1] + f_im * ramp_zy[0]

    def shift_one(j, carry):
        moved[slot_rows(j), :] = jnp.concatenate(shifted_slot(j), axis=0)
        return carry

    def shift_part(q):
        lax.fori_loop(q * 2 * PAIRS, (q + 1) * 2 * PAIRS, shift_one, 0)
        if q == 0:
            moved[slot_rows(0), :] = packed(halves(moved[slot_rows(0), :]), shifted_last())

    for it in range(ITERS):

        def part_steps(q):
            def begin():
                if it == 0:
                    forward_part(q)
                else:
                    shift_part(q)

            def end():
                if q == 0:
                    unpack(it)
                inverse_part(
                    it,
                    q,
                    lambda j: whiten(*slot_of(spec, first_f, j), *slot_of(tmpl.at[it], first_t.at[it], j)),
                    lambda: whiten(*halves(last_f[...]), *halves(last_t[it])),
                )

            steps = sum_steps(it, q, moved if it > 0 else spec)
            return [lambda: (begin(), steps[0]())] + steps[1:-1] + [lambda: (steps[-1](), end())]

        plan = [part_steps(q) for q in range(NQ)]
        for wave in range(NQ + len(plan[0]) - 1):
            for q in range(NQ):
                if 0 <= wave - q < len(plan[q]):
                    plan[q][wave - q]()
        inverse_wait(it)
        shifts = centroid(it)
        make_ramp(shifts)

    for q in range(NQ):
        inverse_part(ITERS, q, shifted_slot, shifted_last)
    inverse_wait(ITERS)
    for z in range(0, SLABS, 2):
        value = cells(ITERS, z)
        for i in range(2):
            out_ref[z + i] = value[:, i * 128 : (i + 1) * 128]
    by_z, by_x, by_y = shifts
    line = jnp.where(lane == 0, by_z, jnp.where(lane == 1, by_x, by_y))
    shift_ref[...] = line[:, 0:3]

    for copy in sends:
        copy.wait_send()

    def finish(q, carry):
        wait_sent(send_f, recv_f, fwd_send, fwd_recv, q)
        for n in range(ITERS + 1):
            wait_sent(send_i.at[n], recv_i.at[n], inv_send.at[n], inv_recv.at[n], q)
        return carry

    lax.fori_loop(0, NQ, finish, 0)
    for it in range(ITERS):

        def done(i, carry):
            d = (s + i) % SPACE
            pltpu.make_async_remote_copy(
                src_ref=stats_out.at[it],
                dst_ref=stats_in.at[it, s],
                send_sem=st_send.at[it, d],
                recv_sem=st_recv.at[it, s],
                device_id={"space": d},
                device_id_type=MESH,
            ).wait_send()
            return carry

        lax.fori_loop(1, SPACE, done, 0)


def body(volumes):
    consts = [jnp.asarray(table) for table in tables()]
    vmem = pl.BlockSpec(memory_space=pltpu.VMEM)
    hbm = pl.BlockSpec(memory_space=pltpu.HBM)
    dma = pltpu.SemaphoreType.DMA
    slots = SLOTS * 2 * Z
    corrected, shifts = pl.pallas_call(
        kernel,
        out_shape=(
            jax.ShapeDtypeStruct((SLABS, X, Y), F32),
            jax.ShapeDtypeStruct((1, 3), F32),
        ),
        in_specs=[hbm] * (1 + len(consts)),
        out_specs=(vmem, vmem),
        scratch_shapes=[
            pltpu.VMEM((SLABS, X, Y), F32),
            *[pltpu.VMEM(table.shape, BF16) for table in consts],
            pltpu.VMEM((ROWS, 128), F32),
            pltpu.VMEM((ROWS, 128), F32),
            pltpu.VMEM((slots, 128), F32),
            pltpu.VMEM((slots, 128), F32),
            pltpu.VMEM((2 * Z, 128), F32),
            pltpu.VMEM((2 * Z, 128), F32),
            pltpu.VMEM((ITERS, 2 * Z, 128), F32),
            pltpu.VMEM((ITERS, 2 * Z, 128), F32),
            pltpu.VMEM((ITERS, NQ, HALF, 128), F32),
            pltpu.VMEM((ITERS, NQ, HALF, 128), F32),
            pltpu.VMEM((ITERS, NQ, 7, UNIT, 128), F32),
            pltpu.VMEM((ITERS, NQ, 3, UNIT, 128), F32),
            pltpu.VMEM((ITERS, slots, 128), F32),
            pltpu.VMEM((ITERS + 1, ROWS, 128), F32),
            pltpu.VMEM((ITERS + 1, ROWS, 128), F32),
            pltpu.VMEM((SLABS, X, 128), F32),
            pltpu.VMEM((ITERS, 8, 128), F32),
            pltpu.VMEM((ITERS, SPACE, 8, 128), F32),
            pltpu.VMEM((2, Z, 128), F32),
            pltpu.VMEM((2, SLOTS, 8, 128), F32),
            dma((1 + len(consts),)),
            dma((NQ, SPACE)), dma((NQ, SPACE)),
            dma((ITERS + 1, NQ, SPACE)), dma((ITERS + 1, NQ, SPACE)),
            dma((ITERS, SPACE)), dma((ITERS, SPACE)),
            dma((ITERS, NQ)), dma((ITERS, NQ)),
            dma((ITERS, NQ, 7)), dma((ITERS, NQ, 7)),
            dma((ITERS, NQ, 7)), dma((ITERS, NQ, 7)),
            dma((ITERS, NQ)), dma((ITERS, NQ)),
        ],
        compiler_params=pltpu.CompilerParams(
            collective_id=0, has_side_effects=True, vmem_limit_bytes=56 * 2**20
        ),
        name="register",
    )(volumes[0], *consts)
    return corrected[None], shifts


def solution(mesh):
    in_specs = (P("tm", "space", None, None),)
    out_specs = (P("tm", "space", None, None), P("tm", None))
    return jax.shard_map(body, mesh=mesh, in_specs=in_specs, out_specs=out_specs, check_vma=False)
```

```python
import functools
import math

import jax
import jax.numpy as jnp
import ml_dtypes
import numpy as np
from jax import lax
from jax.experimental import pallas as pl
from jax.experimental.pallas import tpu as pltpu
from jax.sharding import PartitionSpec as P

X = 512
Y = 128
Z = 64
ITERS = 2
FRAMES = 16
SHARPNESS = 256.0
FLOOR = 0.05 * (X * Y * Z)

SPACE = 16
CHIPS = 8
SLABS = Z // SPACE
SLOTS = X // 2 // SPACE
ROWS = SPACE * SLOTS * 8
MSG = SLOTS * 8
NQ = 4
PART = MSG // NQ
HALF = SLOTS // NQ * Z
UNIT = HALF // CHIPS
GROUP = 4
GROUPS = SLOTS // NQ // GROUP
FIRST_SUMS = ((2, 1), (4, 1), (-3, -1), (-1, -1))
MERGED = (1, 3, -2)
MEANS = (-1, -3, 2, 1)
PASSED = ((1, -1), (3, -1), (-2, 1))
LAST_MEANS = (-1, 2, 4, -3)
REACHED = (1, -1, 2, -2, 3, -3)
SPACING = (3.0, 1.0)
STEP = 3.5
MESH = pl.DeviceIdType.MESH
F32 = jnp.float32
BF16 = jnp.bfloat16


def tables():
    def angles(n, rows, columns):
        return 2.0 * np.pi * ((rows[:, None] * columns[None, :]) % n) / n

    half = X // 2
    a = angles(X, np.arange(half), np.arange(X))
    sign = (-1.0) ** np.arange(X)
    cos_x, sin_x = np.cos(a), np.sin(a)
    im = -sin_x
    im[0] = sign
    forward_x = np.concatenate([cos_x, im])
    weight = np.full((X, 1), 2.0)
    weight[0] = weight[half] = 1.0
    inverse_x = (forward_x * weight).T / (X * Y * Z)

    a = angles(Y, np.arange(Y), np.arange(Y))
    c, s = np.cos(a), np.sin(a)
    forward_y = np.block([[c, -s], [s, c]])
    inverse_y = np.block([[c, s], [-s, c]])

    a = angles(Z, np.arange(Z), np.arange(Z))
    c, s = np.cos(a), np.sin(a)
    forward_z = np.block([[c, s], [-s, c]])
    inverse_z = np.block([[c, -s], [s, c]])
    order = np.arange(2 * Z).reshape(2, SPACE, SLABS).transpose(1, 0, 2).reshape(-1)
    forward_z = forward_z[:, order]
    inverse_z = inverse_z[order, :]

    out = []
    for table in (forward_x, inverse_x, forward_y, inverse_y, forward_z, inverse_z):
        high = table.astype(np.float32).astype(ml_dtypes.bfloat16)
        low = (table - high.astype(np.float64)).astype(np.float32).astype(ml_dtypes.bfloat16)
        out.append(np.stack([high, low]))
    flips = [np.zeros((n, n), ml_dtypes.bfloat16) for n in (Z, Y)]
    for flip in flips:
        flip[np.arange(len(flip)), -np.arange(len(flip))] = 1.0
    return out + flips


def split(value):
    high = value.astype(BF16)
    return high, (value - high.astype(F32)).astype(BF16)


def dot(a, b):
    return jnp.dot(a, b, preferred_element_type=F32)


def table_dot(table, data):
    data_high, data_low = split(data)
    return dot(table[0], data_high) + (dot(table[0], data_low) + dot(table[1], data_high))


def dot_table(data, table):
    data_high, data_low = split(data)
    return dot(data_high, table[0]) + (dot(data_low, table[0]) + dot(data_high, table[1]))


def rows_of(start, count):
    return pl.ds(pl.multiple_of(start, 8), count)


def signed(index, n):
    wrapped = jnp.where(index < n // 2, index, index - n)
    return jnp.where(index == n // 2, 0, wrapped).astype(F32)


def kernel(
    v_hbm, fx_hbm, ix_hbm, fy_hbm, iy_hbm, fz_hbm, iz_hbm, flip_z_hbm, flip_y_hbm,
    out_ref, shift_ref,
    v_ref, fx, ix, fy, iy, fz, iz, flip_z, flip_y,
    send_f, recv_f, spec, moved, first_f, last_f, first_t, last_t, other, pair,
    sums_in, sums_out, tmpl,
    send_i, recv_i, scores, stats_out, stats_in, ramp_zy, ramp_x,
    load_sem, fwd_send, fwd_recv, inv_send, inv_recv, st_send, st_recv,
    oc_send, oc_recv, sum_send, sum_recv, mean_send, mean_recv, go_send, go_recv,
):
    s = lax.axis_index("space")
    t = lax.axis_index("tm")
    core = t % 2
    chip = t // 2
    mate = chip * 2 + 1 - core

    loads = [
        pltpu.make_async_copy(source, target, load_sem.at[i])
        for i, (source, target) in enumerate(
            [
                (fx_hbm, fx), (v_hbm, v_ref), (fz_hbm, fz), (fy_hbm, fy), (iy_hbm, iy),
                (iz_hbm, iz), (flip_z_hbm, flip_z), (flip_y_hbm, flip_y), (ix_hbm, ix),
            ]
        )
    ]
    for copy in loads:
        copy.start()

    barrier = pltpu.get_barrier_semaphore()

    def greet(i, carry):
        pl.semaphore_signal(barrier, inc=1, device_id={"space": (s + i) % SPACE}, device_id_type=MESH)
        return carry

    lax.fori_loop(1, SPACE, greet, 0)
    for offset in REACHED:
        member = ((chip + CHIPS + offset) % CHIPS) * 2 + core
        pl.semaphore_signal(barrier, inc=1, device_id={"tm": member}, device_id_type=MESH)
    pl.semaphore_signal(barrier, inc=1, device_id={"tm": mate}, device_id_type=MESH)

    row = lax.broadcasted_iota(jnp.int32, (2 * Z, 128), 0)
    first_part = (row // SLABS) % 2 == 0

    def to_space(source, start, target, target_start, send_sem, recv_sem, device, count):
        return pltpu.make_async_remote_copy(
            src_ref=source.at[rows_of(start, count)],
            dst_ref=target.at[rows_of(target_start, count)],
            send_sem=send_sem,
            recv_sem=recv_sem,
            device_id={"space": device},
            device_id_type=MESH,
        )

    for copy in loads[:2]:
        copy.wait()

    for z in range(0, SLABS, 2):
        data = jnp.concatenate([v_ref[z], v_ref[z + 1]], axis=1)
        result = table_dot(fx, data)
        for i in range(2):
            for part in range(2):
                send_f[pl.ds(part * SLABS + z + i, X // 2, stride=8), :] = result[
                    part * (X // 2) : (part + 1) * (X // 2), i * 128 : (i + 1) * 128
                ]

    pl.semaphore_wait(barrier, SPACE + len(REACHED))

    def exchange_part(source, target, send_sem, recv_sem, q):
        def one(i, carry):
            d = (s + i) % SPACE
            to_space(
                source, d * MSG + q * PART, target, s * MSG + q * PART,
                send_sem.at[q, d], recv_sem.at[q, s], d, PART,
            ).start()
            return carry

        lax.fori_loop(1, SPACE, one, 0)
        mine = rows_of(s * MSG + q * PART, PART)
        target[mine, :] = source[mine, :]

    def wait_part(source, target, send_sem, recv_sem, q):
        def one(i, carry):
            d = (s + i) % SPACE
            to_space(
                source, d * MSG + q * PART, target, d * MSG + q * PART,
                send_sem.at[q, d], recv_sem.at[q, d], d, PART,
            ).wait_recv()
            return carry

        lax.fori_loop(1, SPACE, one, 0)

    def wait_sent(source, target, send_sem, recv_sem, q):
        def one(i, carry):
            d = (s + i) % SPACE
            to_space(
                source, d * MSG + q * PART, target, s * MSG + q * PART,
                send_sem.at[q, d], recv_sem.at[q, s], d, PART,
            ).wait_send()
            return carry

        lax.fori_loop(1, SPACE, one, 0)

    def send_all(q, carry):
        exchange_part(send_f, recv_f, fwd_send, fwd_recv, q)
        return carry

    lax.fori_loop(0, NQ, send_all, 0)
    for copy in loads[2:]:
        copy.wait()

    def load_slot(j):
        return jnp.concatenate([recv_f[rows_of(d * MSG + j * 8, 8), :] for d in range(SPACE)], axis=0)

    def complex_rows(value):
        return jnp.concatenate([value[:Z], value[Z:]], axis=1)

    def part_rows(value):
        return jnp.concatenate([value[:, :128], value[:, 128:]], axis=0)

    def spectrum_of(slots):
        zed = table_dot(fz, jnp.concatenate(slots, axis=1))
        lines = [complex_rows(zed[:, i * 128 : (i + 1) * 128]) for i in range(len(slots))]
        freq = dot_table(jnp.concatenate(lines, axis=0), fy)
        return [part_rows(freq[i * Z : (i + 1) * Z]) for i in range(len(slots))]

    def slot_rows(j):
        return rows_of(j * 2 * Z, 2 * Z)

    def spectrum_group(i, carry):
        group = [GROUP * i + k for k in range(GROUP)]
        for j, value in zip(group, spectrum_of([load_slot(j) for j in group])):
            spec[slot_rows(j), :] = value
        return carry

    owner = jnp.where(s == 0, 1.0, 0.0)

    def forward_part(q):
        wait_part(send_f, recv_f, fwd_send, fwd_recv, q)
        lax.fori_loop(q * GROUPS, (q + 1) * GROUPS, spectrum_group, 0)
        if q == 0:
            slot = load_slot(0)
            keep = jnp.where(first_part, 1.0, 1.0 - owner)
            rolled = jnp.concatenate([slot[SLABS:], slot[:SLABS]], axis=0)
            first_f[...], last_f[...] = spectrum_of(
                [slot * keep, rolled * jnp.where(first_part, owner, 0.0)]
            )

    sends = []

    def to_tm(source, target, send_sem, recv_sem, device):
        return pltpu.make_async_remote_copy(
            src_ref=source,
            dst_ref=target,
            send_sem=send_sem,
            recv_sem=recv_sem,
            device_id={"tm": device},
            device_id_type=MESH,
        )

    def start(copy):
        copy.start()
        sends.append(copy)

    def half_rows(q, c):
        return rows_of((2 * q + c) * HALF, HALF)

    def sum_steps(it, q, source):
        def pair_unit(i):
            return pair.at[it, q, rows_of((i % CHIPS) * UNIT, UNIT)]

        def mean_unit(i):
            return tmpl.at[it, rows_of((2 * q + core) * HALF + (i % CHIPS) * UNIT, UNIT)]

        def swap():
            return to_tm(source.at[half_rows(q, 1 - core)], other.at[it, q], oc_send.at[it, q], oc_recv.at[it, q], mate)

        def chip_at(offset):
            return ((chip + CHIPS + offset) % CHIPS) * 2 + core

        def sum_copy(outgoing, k, offset):
            return to_tm(outgoing, sums_in.at[it, q, k], sum_send.at[it, q, k], sum_recv.at[it, q, k], chip_at(offset))

        def mean_copy(i, k, offset):
            ref = mean_unit(chip + CHIPS + i)
            return to_tm(ref, ref, mean_send.at[it, q, k], mean_recv.at[it, q, k], chip_at(offset))

        def to_mate(c):
            ref = tmpl.at[it, half_rows(q, c)]
            return to_tm(ref, ref, go_send.at[it, q], go_recv.at[it, q], mate)

        def step_swap():
            start(swap())

        def step_pair():
            swap().wait_recv()
            pair[it, q] = source[half_rows(q, core), :] + other[it, q]
            for k, (i, offset) in enumerate(FIRST_SUMS):
                start(sum_copy(pair_unit(chip + CHIPS + i), k, offset))

        def step_merge():
            for k, i in enumerate(MERGED):
                sum_copy(sums_out.at[it, q, k], k, i).wait_recv()
                sums_out[it, q, k] = pair_unit(chip + CHIPS + i)[...] + sums_in[it, q, k]
                start(sum_copy(sums_out.at[it, q, k], 4 + k, i))

        def step_mean():
            total = pair_unit(chip)[...]
            for k in range(3, 7):
                sum_copy(sums_in.at[it, q, k], k, 1).wait_recv()
                total = total + sums_in[it, q, k]
            tmpl[it, rows_of((2 * q + core) * HALF + chip * UNIT, UNIT), :] = total * (1.0 / FRAMES)
            for k, offset in enumerate(MEANS):
                start(mean_copy(0, k, offset))

        def step_pass():
            for k, (i, offset) in enumerate(PASSED):
                mean_copy(i, k, 1).wait_recv()
                start(mean_copy(i, 4 + k, offset))

        def step_share():
            for k, i in enumerate(LAST_MEANS):
                mean_copy(i, 3 + k, 1).wait_recv()
            start(to_mate(core))

        def step_end():
            to_mate(1 - core).wait_recv()

        return [step_swap, step_pair, step_merge, step_mean, step_pass, step_share, step_end]

    def whiten(f_re, f_im, t_re, t_im):
        p_re = f_re * t_re + f_im * t_im
        p_im = f_im * t_re - f_re * t_im
        scale = lax.rsqrt(jnp.maximum(p_re * p_re + p_im * p_im, FLOOR * FLOOR))
        return p_re * scale, p_im * scale

    def halves(value):
        return value[:Z], value[Z:]

    def slot_of(ref, first, j):
        return halves(jnp.where(j == 0, first[...], ref[slot_rows(j), :]))

    def packed(first, last):
        (f_re, f_im), (l_re, l_im) = first, last
        return jnp.concatenate([f_re - l_im, f_im + l_re], axis=0)

    def flipped(value):
        high, low = split(value)
        value = dot(flip_z[...], high) + dot(flip_z[...], low)
        high, low = split(part_rows(value))
        return halves(dot(high, flip_y[...]) + dot(low, flip_y[...]))

    def unpack(it):
        value = tmpl[it, slot_rows(0), :]
        re, im = halves(value)
        flip_re, flip_im = flipped(complex_rows(value))
        half = 0.5 * owner
        first_t[it] = jnp.concatenate([re - half * (re - flip_re), im - half * (im + flip_im)], axis=0)
        last_t[it] = jnp.concatenate([half * (im + flip_im), half * (flip_re - re)], axis=0)

    def back(values):
        lines = [jnp.concatenate([re, im], axis=1) for re, im in values]
        lines = dot_table(jnp.concatenate(lines, axis=0), iy)
        planes = [part_rows(lines[i * Z : (i + 1) * Z]) for i in range(len(values))]
        return table_dot(iz, jnp.concatenate(planes, axis=1))

    def inverse_part(n, q, slot_values, last_values):
        if q == 0:
            last = back([last_values()])
            last = jnp.concatenate([last[2 * Z - SLABS :], last[: 2 * Z - SLABS]], axis=0)

        def group_back(i, carry):
            group = [GROUP * i + k for k in range(GROUP)]
            planes = back([slot_values(j) for j in group])
            for k, j in enumerate(group):
                value = planes[:, k * 128 : (k + 1) * 128]
                if q == 0 and k == 0:
                    keep = jnp.where(first_part, 1.0, jnp.where(s + j == 0, 0.0, 1.0))
                    value = value * keep + last * (1.0 - keep)
                for d in range(SPACE):
                    send_i[n, rows_of(d * MSG + j * 8, 8), :] = value[8 * d : 8 * d + 8]
            return carry

        lax.fori_loop(q * GROUPS, (q + 1) * GROUPS, group_back, 0)
        exchange_part(send_i.at[n], recv_i.at[n], inv_send.at[n], inv_recv.at[n], q)

    def inverse_wait(n):
        def one(q, carry):
            wait_part(send_i.at[n], recv_i.at[n], inv_send.at[n], inv_recv.at[n], q)
            return carry

        lax.fori_loop(0, NQ, one, 0)

    def cells(n, z):
        columns = []
        for i in range(2):
            parts = [
                recv_i[n, pl.ds(part * SLABS + z + i, X // 2, stride=8), :] for part in range(2)
            ]
            columns.append(jnp.concatenate(parts, axis=0))
        return table_dot(ix, jnp.concatenate(columns, axis=1))

    lane = lax.broadcasted_iota(jnp.int32, (1, 128), 1)

    def centroid(it):
        top = jnp.full((8, 128), -jnp.inf, F32)
        for z in range(0, SLABS, 2):
            value = cells(it, z) * SHARPNESS
            for i in range(2):
                plane = value[:, i * 128 : (i + 1) * 128]
                scores[z + i] = plane
                top = jnp.maximum(top, jnp.max(plane.reshape(X // 8, 8, 128), axis=0))
        top = jnp.max(jnp.max(top, axis=0, keepdims=True), axis=1, keepdims=True)
        step = 128
        x_row = lax.broadcasted_iota(jnp.int32, (step, 128), 0)
        zero = jnp.zeros((8, 128), F32)

        def weigh(i, carry):
            total, by_z, by_x = carry
            z, x = i // (X // step), (i % (X // step)) * step
            weights = jnp.exp(scores[z, rows_of(x, step), :] - top)
            x_at = ((x + x_row + X // 2) % X - X // 2).astype(F32)
            z_at = ((s * SLABS + z + Z // 2) % Z - Z // 2).astype(F32)
            here = jnp.sum(weights.reshape(step // 8, 8, 128), axis=0)
            by_x = by_x + jnp.sum((weights * x_at).reshape(step // 8, 8, 128), axis=0)
            return total + here, by_z + here * z_at, by_x

        total, by_z, by_x = lax.fori_loop(0, SLABS * X // step, weigh, (zero, zero, zero))
        y_at = ((lane + Y // 2) % Y - Y // 2).astype(F32)
        sums = [jnp.sum(value, axis=0, keepdims=True) for value in (total, by_z, by_x)]
        rows = [jnp.broadcast_to(top, (1, 128))] + sums + [sums[0] * y_at, jnp.zeros((3, 128), F32)]
        tile = jnp.concatenate(rows, axis=0)
        stats_out[it] = tile
        stats_in[it, s] = tile

        def stat(i, target, sender):
            d = (s + i) % SPACE
            return pltpu.make_async_remote_copy(
                src_ref=stats_out.at[it],
                dst_ref=stats_in.at[it, s if sender else d],
                send_sem=st_send.at[it, d],
                recv_sem=st_recv.at[it, s if sender else d],
                device_id={"space": d},
                device_id_type=MESH,
            )

        def send(i, carry):
            stat(i, s, True).start()
            return carry

        def receive(i, carry):
            stat(i, s, False).wait_recv()
            return carry

        lax.fori_loop(1, SPACE, send, 0)
        lax.fori_loop(1, SPACE, receive, 0)
        every = stats_in[it]
        tops = every[:, 0:1, :]
        scale = jnp.exp(tops - jnp.max(tops, axis=0, keepdims=True))
        sums = jnp.sum(jnp.sum(every * scale, axis=0), axis=1, keepdims=True)
        return [sums[i : i + 1] / sums[1:2] for i in (2, 3, 4)]

    def make_ramp(shifts):
        by_z, by_x, by_y = shifts
        kz = lax.broadcasted_iota(jnp.int32, (Z, 128), 0)
        ky = lax.broadcasted_iota(jnp.int32, (Z, 128), 1)
        phase = (2.0 * math.pi) * (signed(kz, Z) * (by_z / Z) + signed(ky, Y) * (by_y / Y))
        ramp_zy[0] = jnp.cos(phase)
        ramp_zy[1] = jnp.sin(phase)
        kx = s * SLOTS + lax.broadcasted_iota(jnp.int32, (SLOTS, 128), 0)
        phase = (2.0 * math.pi) * (kx.astype(F32) * (by_x / X))
        cos_x, sin_x = jnp.cos(phase), jnp.sin(phase)
        for j in range(SLOTS):
            ramp_x[0, j] = jnp.broadcast_to(cos_x[j : j + 1], (8, 128))
            ramp_x[1, j] = jnp.broadcast_to(sin_x[j : j + 1], (8, 128))

    def shifted_slot(j):
        cos_x = jnp.concatenate([ramp_x[0, j]] * (Z // 8), axis=0)
        sin_x = jnp.concatenate([ramp_x[1, j]] * (Z // 8), axis=0)
        cosine = ramp_zy[0] * cos_x - ramp_zy[1] * sin_x
        sine = ramp_zy[1] * cos_x + ramp_zy[0] * sin_x
        f_re, f_im = slot_of(spec, first_f, j)
        return f_re * cosine - f_im * sine, f_re * sine + f_im * cosine

    def shifted_last():
        f_re, f_im = halves(last_f[...])
        return f_re * ramp_zy[0] - f_im * ramp_zy[1], f_re * ramp_zy[1] + f_im * ramp_zy[0]

    def shift_one(j, carry):
        moved[slot_rows(j), :] = jnp.concatenate(shifted_slot(j), axis=0)
        return carry

    def shift_part(q):
        lax.fori_loop(q * GROUPS * GROUP, (q + 1) * GROUPS * GROUP, shift_one, 0)
        if q == 0:
            moved[slot_rows(0), :] = packed(halves(moved[slot_rows(0), :]), shifted_last())

    for it in range(ITERS):

        def part_steps(q):
            def begin():
                if it == 0:
                    forward_part(q)
                else:
                    shift_part(q)

            def end():
                if q == 0:
                    unpack(it)
                inverse_part(
                    it,
                    q,
                    lambda j: whiten(*slot_of(spec, first_f, j), *slot_of(tmpl.at[it], first_t.at[it], j)),
                    lambda: whiten(*halves(last_f[...]), *halves(last_t[it])),
                )

            steps = sum_steps(it, q, moved if it > 0 else spec)
            return [lambda: (begin(), steps[0]())] + steps[1:-1] + [lambda: (steps[-1](), end())]

        plan = [
            (SPACING[it] * q + STEP * k, q, step) for q in range(NQ) for k, step in enumerate(part_steps(q))
        ]
        for _, _, step in sorted(plan, key=lambda entry: entry[:2]):
            step()
        inverse_wait(it)
        shifts = centroid(it)
        make_ramp(shifts)

    for q in range(NQ):
        inverse_part(ITERS, q, shifted_slot, shifted_last)
    inverse_wait(ITERS)
    for z in range(0, SLABS, 2):
        value = cells(ITERS, z)
        for i in range(2):
            out_ref[z + i] = value[:, i * 128 : (i + 1) * 128]
    by_z, by_x, by_y = shifts
    line = jnp.where(lane == 0, by_z, jnp.where(lane == 1, by_x, by_y))
    shift_ref[...] = line[:, 0:3]

    for copy in sends:
        copy.wait_send()

    def finish(q, carry):
        wait_sent(send_f, recv_f, fwd_send, fwd_recv, q)
        for n in range(ITERS + 1):
            wait_sent(send_i.at[n], recv_i.at[n], inv_send.at[n], inv_recv.at[n], q)
        return carry

    lax.fori_loop(0, NQ, finish, 0)
    for it in range(ITERS):

        def done(i, carry):
            d = (s + i) % SPACE
            pltpu.make_async_remote_copy(
                src_ref=stats_out.at[it],
                dst_ref=stats_in.at[it, s],
                send_sem=st_send.at[it, d],
                recv_sem=st_recv.at[it, s],
                device_id={"space": d},
                device_id_type=MESH,
            ).wait_send()
            return carry

        lax.fori_loop(1, SPACE, done, 0)


def body(volumes):
    consts = [jnp.asarray(table) for table in tables()]
    vmem = pl.BlockSpec(memory_space=pltpu.VMEM)
    hbm = pl.BlockSpec(memory_space=pltpu.HBM)
    dma = pltpu.SemaphoreType.DMA
    slots = SLOTS * 2 * Z
    corrected, shifts = pl.pallas_call(
        kernel,
        out_shape=(
            jax.ShapeDtypeStruct((SLABS, X, Y), F32),
            jax.ShapeDtypeStruct((1, 3), F32),
        ),
        in_specs=[hbm] * (1 + len(consts)),
        out_specs=(vmem, vmem),
        scratch_shapes=[
            pltpu.VMEM((SLABS, X, Y), F32),
            *[pltpu.VMEM(table.shape, BF16) for table in consts],
            pltpu.VMEM((ROWS, 128), F32),
            pltpu.VMEM((ROWS, 128), F32),
            pltpu.VMEM((slots, 128), F32),
            pltpu.VMEM((slots, 128), F32),
            pltpu.VMEM((2 * Z, 128), F32),
            pltpu.VMEM((2 * Z, 128), F32),
            pltpu.VMEM((ITERS, 2 * Z, 128), F32),
            pltpu.VMEM((ITERS, 2 * Z, 128), F32),
            pltpu.VMEM((ITERS, NQ, HALF, 128), F32),
            pltpu.VMEM((ITERS, NQ, HALF, 128), F32),
            pltpu.VMEM((ITERS, NQ, 7, UNIT, 128), F32),
            pltpu.VMEM((ITERS, NQ, 3, UNIT, 128), F32),
            pltpu.VMEM((ITERS, slots, 128), F32),
            pltpu.VMEM((ITERS + 1, ROWS, 128), F32),
            pltpu.VMEM((ITERS + 1, ROWS, 128), F32),
            pltpu.VMEM((SLABS, X, 128), F32),
            pltpu.VMEM((ITERS, 8, 128), F32),
            pltpu.VMEM((ITERS, SPACE, 8, 128), F32),
            pltpu.VMEM((2, Z, 128), F32),
            pltpu.VMEM((2, SLOTS, 8, 128), F32),
            dma((1 + len(consts),)),
            dma((NQ, SPACE)), dma((NQ, SPACE)),
            dma((ITERS + 1, NQ, SPACE)), dma((ITERS + 1, NQ, SPACE)),
            dma((ITERS, SPACE)), dma((ITERS, SPACE)),
            dma((ITERS, NQ)), dma((ITERS, NQ)),
            dma((ITERS, NQ, 7)), dma((ITERS, NQ, 7)),
            dma((ITERS, NQ, 7)), dma((ITERS, NQ, 7)),
            dma((ITERS, NQ)), dma((ITERS, NQ)),
        ],
        compiler_params=pltpu.CompilerParams(
            collective_id=0, has_side_effects=True, vmem_limit_bytes=56 * 2**20
        ),
        name="register",
    )(volumes[0], *consts)
    return corrected[None], shifts


def solution(mesh):
    in_specs = (P("tm", "space", None, None),)
    out_specs = (P("tm", "space", None, None), P("tm", None))
    return jax.shard_map(body, mesh=mesh, in_specs=in_specs, out_specs=out_specs, check_vma=False)
```

```python
import functools
import math

import jax
import jax.numpy as jnp
import ml_dtypes
import numpy as np
from jax import lax
from jax.experimental import pallas as pl
from jax.experimental.pallas import tpu as pltpu
from jax.sharding import PartitionSpec as P

X = 512
Y = 128
Z = 64
ITERS = 2
FRAMES = 16
SHARPNESS = 256.0
FLOOR = 0.05 * (X * Y * Z)

SPACE = 16
CHIPS = 8
SLABS = Z // SPACE
SLOTS = X // 2 // SPACE
ROWS = SPACE * SLOTS * 8
MSG = SLOTS * 8
NQ = 4
PART = MSG // NQ
HALF = SLOTS // NQ * Z
UNIT = HALF // CHIPS
GROUP = 4
GROUPS = SLOTS // NQ // GROUP
FIRST_SUMS = ((2, 1), (4, 1), (-3, -1), (-1, -1))
MERGED = (1, 3, -2)
MEANS = (-1, -3, 2, 1)
PASSED = ((1, -1), (3, -1), (-2, 1))
LAST_MEANS = (-1, 2, 4, -3)
REACHED = (1, -1, 2, -2, 3, -3)
SPACING = (3.0, 1.0)
STEP = 3.5
MESH = pl.DeviceIdType.MESH
F32 = jnp.float32
BF16 = jnp.bfloat16


def tables():
    def angles(n, rows, columns):
        return 2.0 * np.pi * ((rows[:, None] * columns[None, :]) % n) / n

    half = X // 2
    a = angles(X, np.arange(half), np.arange(X))
    sign = (-1.0) ** np.arange(X)
    cos_x, sin_x = np.cos(a), np.sin(a)
    im = -sin_x
    im[0] = sign
    forward_x = np.concatenate([cos_x, im])
    weight = np.full((X, 1), 2.0)
    weight[0] = weight[half] = 1.0
    inverse_x = (forward_x * weight).T / (X * Y * Z)

    a = angles(Y, np.arange(Y), np.arange(Y))
    c, s = np.cos(a), np.sin(a)
    forward_y = np.block([[c, -s], [s, c]])
    inverse_y = np.block([[c, s], [-s, c]])

    a = angles(Z, np.arange(Z), np.arange(Z))
    c, s = np.cos(a), np.sin(a)
    forward_z = np.block([[c, s], [-s, c]])
    inverse_z = np.block([[c, -s], [s, c]])
    order = np.arange(2 * Z).reshape(2, SPACE, SLABS).transpose(1, 0, 2).reshape(-1)
    forward_z = forward_z[:, order]
    inverse_z = inverse_z[order, :]

    slots = np.arange(X // 2).reshape(SPACE, 2, NQ // 2, SLOTS // NQ).transpose(1, 2, 0, 3).reshape(2, 1, -1)
    columns = slots + np.arange(2)[None, :, None] * (X // 2)

    def two(table):
        high = table.astype(np.float32).astype(ml_dtypes.bfloat16)
        return high, (table - high.astype(np.float64)).astype(np.float32).astype(ml_dtypes.bfloat16)

    def block(table):
        high, low = two(table)
        return np.concatenate(
            [np.concatenate([high, high], axis=1), np.concatenate([low, np.zeros_like(low)], axis=1)]
        )

    out = [
        np.concatenate(two(forward_x)),
        np.stack([np.concatenate(two(inverse_x[:, half.reshape(-1)])) for half in columns]),
        np.stack(two(forward_y)),
        np.stack(two(inverse_y)),
        block(forward_z),
        block(inverse_z),
    ]
    flips = [np.zeros((n, n), ml_dtypes.bfloat16) for n in (Z, Y)]
    for flip in flips:
        flip[np.arange(len(flip)), -np.arange(len(flip))] = 1.0
    return out + flips


def split(value):
    high = value.astype(BF16)
    return high, (value - high.astype(F32)).astype(BF16)


def dot(a, b):
    return jnp.dot(a, b, preferred_element_type=F32)


def x_dot(table, data):
    n = table.shape[0] // 2
    data_high, data_low = split(data)
    both = dot(table, data_high)
    return both[:n] + (both[n:] + dot(table[:n], data_low))


def z_dot(table, data):
    n = table.shape[0] // 2
    both = dot(table, jnp.concatenate(split(data), axis=0))
    return both[:n] + both[n:]


def dot_y(data, table):
    n = data.shape[0]
    data_high, data_low = split(data)
    both = dot(jnp.concatenate([data_high, data_low], axis=0), table[0])
    return both[:n] + (both[n:] + dot(data_high, table[1]))


def rows_of(start, count):
    return pl.ds(start if isinstance(start, int) else pl.multiple_of(start, 8), count)


def signed(index, n):
    wrapped = jnp.where(index < n // 2, index, index - n)
    return jnp.where(index == n // 2, 0, wrapped).astype(F32)


def kernel(
    v_hbm, fx_hbm, ix_hbm, fy_hbm, iy_hbm, fz_hbm, iz_hbm, flip_z_hbm, flip_y_hbm,
    out_ref, shift_ref,
    v_ref, fx, ix, fy, iy, fz, iz, flip_z, flip_y,
    send_f, recv_f, spec, moved, first_f, last_f, first_t, last_t, other, pair,
    sums_in, sums_out, tmpl,
    send_i, recv_i, scores, stats_out, stats_in, ramp_zy, ramp_x,
    load_sem, fwd_send, fwd_recv, inv_send, inv_recv, st_send, st_recv,
    oc_send, oc_recv, sum_send, sum_recv, mean_send, mean_recv, go_send, go_recv,
):
    s = lax.axis_index("space")
    t = lax.axis_index("tm")
    core = t % 2
    chip = t // 2
    mate = chip * 2 + 1 - core

    loads = [
        pltpu.make_async_copy(source, target, load_sem.at[i])
        for i, (source, target) in enumerate(
            [
                (fx_hbm, fx), (v_hbm, v_ref), (fz_hbm, fz), (fy_hbm, fy), (iy_hbm, iy),
                (iz_hbm, iz), (flip_z_hbm, flip_z), (flip_y_hbm, flip_y), (ix_hbm, ix),
            ]
        )
    ]
    for copy in loads:
        copy.start()

    barrier = pltpu.get_barrier_semaphore()

    def greet(i, carry):
        pl.semaphore_signal(barrier, inc=1, device_id={"space": (s + i) % SPACE}, device_id_type=MESH)
        return carry

    lax.fori_loop(1, SPACE, greet, 0)
    for offset in REACHED:
        member = ((chip + CHIPS + offset) % CHIPS) * 2 + core
        pl.semaphore_signal(barrier, inc=1, device_id={"tm": member}, device_id_type=MESH)
    pl.semaphore_signal(barrier, inc=1, device_id={"tm": mate}, device_id_type=MESH)

    row = lax.broadcasted_iota(jnp.int32, (2 * Z, 128), 0)
    first_part = (row // SLABS) % 2 == 0

    def to_space(source, start, target, target_start, send_sem, recv_sem, device, count):
        return pltpu.make_async_remote_copy(
            src_ref=source.at[rows_of(start, count)],
            dst_ref=target.at[rows_of(target_start, count)],
            send_sem=send_sem,
            recv_sem=recv_sem,
            device_id={"space": device},
            device_id_type=MESH,
        )

    for copy in loads[:2]:
        copy.wait()

    for z in range(0, SLABS, 2):
        data = jnp.concatenate([v_ref[z], v_ref[z + 1]], axis=1)
        result = x_dot(fx[...], data)
        for i in range(2):
            for part in range(2):
                send_f[pl.ds(part * SLABS + z + i, X // 2, stride=8), :] = result[
                    part * (X // 2) : (part + 1) * (X // 2), i * 128 : (i + 1) * 128
                ]

    pl.semaphore_wait(barrier, SPACE + len(REACHED))

    def by_device(device, q):
        return device * MSG + q * PART

    def by_part(device, q):
        return (q * SPACE + device) * PART

    def exchange_part(source, target, send_sem, recv_sem, q, place):
        def one(i, carry):
            d = (s + i) % SPACE
            to_space(
                source, by_device(d, q), target, place(s, q), send_sem.at[q, d], recv_sem.at[q, s], d, PART
            ).start()
            return carry

        lax.fori_loop(1, SPACE, one, 0)
        target[rows_of(place(s, q), PART), :] = source[rows_of(by_device(s, q), PART), :]

    def wait_part(source, target, send_sem, recv_sem, q, place):
        def one(i, carry):
            d = (s + i) % SPACE
            to_space(
                source, by_device(d, q), target, place(d, q), send_sem.at[q, d], recv_sem.at[q, d], d, PART
            ).wait_recv()
            return carry

        lax.fori_loop(1, SPACE, one, 0)

    def wait_sent(source, target, send_sem, recv_sem, q, place):
        def one(i, carry):
            d = (s + i) % SPACE
            to_space(
                source, by_device(d, q), target, place(s, q), send_sem.at[q, d], recv_sem.at[q, s], d, PART
            ).wait_send()
            return carry

        lax.fori_loop(1, SPACE, one, 0)

    def send_all(q, carry):
        exchange_part(send_f, recv_f, fwd_send, fwd_recv, q, by_device)
        return carry

    lax.fori_loop(0, NQ, send_all, 0)
    for copy in loads[2:]:
        copy.wait()

    def load_slot(j):
        return jnp.concatenate([recv_f[rows_of(d * MSG + j * 8, 8), :] for d in range(SPACE)], axis=0)

    def complex_rows(value):
        return jnp.concatenate([value[:Z], value[Z:]], axis=1)

    def part_rows(value):
        return jnp.concatenate([value[:, :128], value[:, 128:]], axis=0)

    def spectrum_of(slots):
        zed = z_dot(fz[...], jnp.concatenate(slots, axis=1))
        lines = [complex_rows(zed[:, i * 128 : (i + 1) * 128]) for i in range(len(slots))]
        freq = dot_y(jnp.concatenate(lines, axis=0), fy)
        return [part_rows(freq[i * Z : (i + 1) * Z]) for i in range(len(slots))]

    def slot_rows(j):
        return rows_of(j * 2 * Z, 2 * Z)

    def groups(q):
        return [[GROUP * i + k for k in range(GROUP)] for i in range(q * GROUPS, (q + 1) * GROUPS)]

    owner = jnp.where(s == 0, 1.0, 0.0)

    def forward_part(q):
        wait_part(send_f, recv_f, fwd_send, fwd_recv, q, by_device)
        for group in groups(q):
            for j, value in zip(group, spectrum_of([load_slot(j) for j in group])):
                spec[slot_rows(j), :] = value
        if q == 0:
            slot = load_slot(0)
            keep = jnp.where(first_part, 1.0, 1.0 - owner)
            rolled = jnp.concatenate([slot[SLABS:], slot[:SLABS]], axis=0)
            first_f[...], last_f[...] = spectrum_of(
                [slot * keep, rolled * jnp.where(first_part, owner, 0.0)]
            )

    sends = []

    def to_tm(source, target, send_sem, recv_sem, device):
        return pltpu.make_async_remote_copy(
            src_ref=source,
            dst_ref=target,
            send_sem=send_sem,
            recv_sem=recv_sem,
            device_id={"tm": device},
            device_id_type=MESH,
        )

    def start(copy):
        copy.start()
        sends.append(copy)

    def half_rows(q, c):
        return rows_of((2 * q + c) * HALF, HALF)

    def sum_steps(it, q, source):
        def pair_unit(i):
            return pair.at[it, q, rows_of((i % CHIPS) * UNIT, UNIT)]

        def mean_unit(i):
            return tmpl.at[it, rows_of((2 * q + core) * HALF + (i % CHIPS) * UNIT, UNIT)]

        def swap():
            return to_tm(source.at[half_rows(q, 1 - core)], other.at[it, q], oc_send.at[it, q], oc_recv.at[it, q], mate)

        def chip_at(offset):
            return ((chip + CHIPS + offset) % CHIPS) * 2 + core

        def sum_copy(outgoing, k, offset):
            return to_tm(outgoing, sums_in.at[it, q, k], sum_send.at[it, q, k], sum_recv.at[it, q, k], chip_at(offset))

        def mean_copy(i, k, offset):
            ref = mean_unit(chip + CHIPS + i)
            return to_tm(ref, ref, mean_send.at[it, q, k], mean_recv.at[it, q, k], chip_at(offset))

        def to_mate(c):
            ref = tmpl.at[it, half_rows(q, c)]
            return to_tm(ref, ref, go_send.at[it, q], go_recv.at[it, q], mate)

        def step_swap():
            start(swap())

        def step_pair():
            swap().wait_recv()
            pair[it, q] = source[half_rows(q, core), :] + other[it, q]
            for k, (i, offset) in enumerate(FIRST_SUMS):
                start(sum_copy(pair_unit(chip + CHIPS + i), k, offset))

        def step_merge():
            for k, i in enumerate(MERGED):
                sum_copy(sums_out.at[it, q, k], k, i).wait_recv()
                sums_out[it, q, k] = pair_unit(chip + CHIPS + i)[...] + sums_in[it, q, k]
                start(sum_copy(sums_out.at[it, q, k], 4 + k, i))

        def step_mean():
            total = pair_unit(chip)[...]
            for k in range(3, 7):
                sum_copy(sums_in.at[it, q, k], k, 1).wait_recv()
                total = total + sums_in[it, q, k]
            tmpl[it, rows_of((2 * q + core) * HALF + chip * UNIT, UNIT), :] = total * (1.0 / FRAMES)
            for k, offset in enumerate(MEANS):
                start(mean_copy(0, k, offset))

        def step_pass():
            for k, (i, offset) in enumerate(PASSED):
                mean_copy(i, k, 1).wait_recv()
                start(mean_copy(i, 4 + k, offset))

        def step_share():
            for k, i in enumerate(LAST_MEANS):
                mean_copy(i, 3 + k, 1).wait_recv()
            start(to_mate(core))

        def step_end():
            to_mate(1 - core).wait_recv()

        return [step_swap, step_pair, step_merge, step_mean, step_pass, step_share, step_end]

    def whiten(f_re, f_im, t_re, t_im):
        p_re = f_re * t_re + f_im * t_im
        p_im = f_im * t_re - f_re * t_im
        scale = lax.rsqrt(jnp.maximum(p_re * p_re + p_im * p_im, FLOOR * FLOOR))
        return p_re * scale, p_im * scale

    def halves(value):
        return value[:Z], value[Z:]

    def slot_of(ref, first, j):
        return halves(first[...] if j == 0 else ref[slot_rows(j), :])

    def packed(first, last):
        (f_re, f_im), (l_re, l_im) = first, last
        return jnp.concatenate([f_re - l_im, f_im + l_re], axis=0)

    def flipped(value):
        high, low = split(value)
        value = dot(flip_z[...], high) + dot(flip_z[...], low)
        high, low = split(part_rows(value))
        return halves(dot(high, flip_y[...]) + dot(low, flip_y[...]))

    def unpack(it):
        value = tmpl[it, slot_rows(0), :]
        re, im = halves(value)
        flip_re, flip_im = flipped(complex_rows(value))
        half = 0.5 * owner
        first_t[it] = jnp.concatenate([re - half * (re - flip_re), im - half * (im + flip_im)], axis=0)
        last_t[it] = jnp.concatenate([half * (im + flip_im), half * (flip_re - re)], axis=0)

    def back(values):
        lines = [jnp.concatenate([re, im], axis=1) for re, im in values]
        lines = dot_y(jnp.concatenate(lines, axis=0), iy)
        planes = [part_rows(lines[i * Z : (i + 1) * Z]) for i in range(len(values))]
        return z_dot(iz[...], jnp.concatenate(planes, axis=1))

    def inverse_part(n, q, slot_values, last_values):
        if q == 0:
            last = back([last_values()])
            last = jnp.concatenate([last[2 * Z - SLABS :], last[: 2 * Z - SLABS]], axis=0)

        for group in groups(q):
            planes = back([slot_values(j) for j in group])
            for k, j in enumerate(group):
                value = planes[:, k * 128 : (k + 1) * 128]
                if j == 0:
                    keep = jnp.where(first_part, 1.0, 1.0 - owner)
                    value = value * keep + last * (1.0 - keep)
                for d in range(SPACE):
                    send_i[n, rows_of(d * MSG + j * 8, 8), :] = value[8 * d : 8 * d + 8]
        exchange_part(send_i.at[n], recv_i.at[n], inv_send.at[n], inv_recv.at[n], q, by_part)

    def inverse_x(n, target):
        count = ROWS // 16

        def wait_one(q, carry):
            wait_part(send_i.at[n], recv_i.at[n], inv_send.at[n], inv_recv.at[n], q, by_part)
            return carry

        for half in range(2):
            lax.fori_loop(half * (NQ // 2), (half + 1) * (NQ // 2), wait_one, 0)
            for z in range(0, SLABS, 2):
                columns = []
                for i in range(2):
                    parts = [
                        recv_i[n, pl.ds(half * count * 8 + part * SLABS + z + i, count, stride=8), :]
                        for part in range(2)
                    ]
                    columns.append(jnp.concatenate(parts, axis=0))
                value = x_dot(ix[half], jnp.concatenate(columns, axis=1))
                for i in range(2):
                    plane = value[:, i * 128 : (i + 1) * 128]
                    target[z + i] = plane if half == 0 else target[z + i] + plane

    lane = lax.broadcasted_iota(jnp.int32, (1, 128), 1)

    def centroid(it):
        top = jnp.full((8, 128), -jnp.inf, F32)
        inverse_x(it, scores)
        for z in range(SLABS):
            top = jnp.maximum(top, jnp.max(scores[z].reshape(X // 8, 8, 128), axis=0))
        top = top * SHARPNESS
        top = jnp.max(jnp.max(top, axis=0, keepdims=True), axis=1, keepdims=True)
        step = 128
        x_row = lax.broadcasted_iota(jnp.int32, (step, 128), 0)
        zero = jnp.zeros((8, 128), F32)

        def weigh(i, carry):
            total, by_z, by_x = carry
            z, x = i // (X // step), (i % (X // step)) * step
            weights = jnp.exp(scores[z, rows_of(x, step), :] * SHARPNESS - top)
            x_at = ((x + x_row + X // 2) % X - X // 2).astype(F32)
            z_at = ((s * SLABS + z + Z // 2) % Z - Z // 2).astype(F32)
            here = jnp.sum(weights.reshape(step // 8, 8, 128), axis=0)
            by_x = by_x + jnp.sum((weights * x_at).reshape(step // 8, 8, 128), axis=0)
            return total + here, by_z + here * z_at, by_x

        total, by_z, by_x = lax.fori_loop(0, SLABS * X // step, weigh, (zero, zero, zero))
        y_at = ((lane + Y // 2) % Y - Y // 2).astype(F32)
        sums = [jnp.sum(value, axis=0, keepdims=True) for value in (total, by_z, by_x)]
        rows = [jnp.broadcast_to(top, (1, 128))] + sums + [sums[0] * y_at, jnp.zeros((3, 128), F32)]
        tile = jnp.concatenate(rows, axis=0)
        stats_out[it] = tile
        stats_in[it, s] = tile

        def stat(i, target, sender):
            d = (s + i) % SPACE
            return pltpu.make_async_remote_copy(
                src_ref=stats_out.at[it],
                dst_ref=stats_in.at[it, s if sender else d],
                send_sem=st_send.at[it, d],
                recv_sem=st_recv.at[it, s if sender else d],
                device_id={"space": d},
                device_id_type=MESH,
            )

        def send(i, carry):
            stat(i, s, True).start()
            return carry

        def receive(i, carry):
            stat(i, s, False).wait_recv()
            return carry

        lax.fori_loop(1, SPACE, send, 0)
        lax.fori_loop(1, SPACE, receive, 0)
        every = stats_in[it]
        tops = every[:, 0:1, :]
        scale = jnp.exp(tops - jnp.max(tops, axis=0, keepdims=True))
        sums = jnp.sum(jnp.sum(every * scale, axis=0), axis=1, keepdims=True)
        return [sums[i : i + 1] / sums[1:2] for i in (2, 3, 4)]

    def make_ramp(shifts):
        by_z, by_x, by_y = shifts
        kz = lax.broadcasted_iota(jnp.int32, (Z, 128), 0)
        ky = lax.broadcasted_iota(jnp.int32, (Z, 128), 1)
        phase = (2.0 * math.pi) * (signed(kz, Z) * (by_z / Z) + signed(ky, Y) * (by_y / Y))
        ramp_zy[0] = jnp.cos(phase)
        ramp_zy[1] = jnp.sin(phase)
        kx = s * SLOTS + lax.broadcasted_iota(jnp.int32, (SLOTS, 128), 0)
        phase = (2.0 * math.pi) * (kx.astype(F32) * (by_x / X))
        cos_x, sin_x = jnp.cos(phase), jnp.sin(phase)
        for j in range(SLOTS):
            ramp_x[0, j] = jnp.broadcast_to(cos_x[j : j + 1], (8, 128))
            ramp_x[1, j] = jnp.broadcast_to(sin_x[j : j + 1], (8, 128))

    def shifted_slot(j):
        cos_x = jnp.concatenate([ramp_x[0, j]] * (Z // 8), axis=0)
        sin_x = jnp.concatenate([ramp_x[1, j]] * (Z // 8), axis=0)
        cosine = ramp_zy[0] * cos_x - ramp_zy[1] * sin_x
        sine = ramp_zy[1] * cos_x + ramp_zy[0] * sin_x
        f_re, f_im = slot_of(spec, first_f, j)
        return f_re * cosine - f_im * sine, f_re * sine + f_im * cosine

    def shifted_last():
        f_re, f_im = halves(last_f[...])
        return f_re * ramp_zy[0] - f_im * ramp_zy[1], f_re * ramp_zy[1] + f_im * ramp_zy[0]

    def shift_part(q):
        for group in groups(q):
            for j in group:
                moved[slot_rows(j), :] = jnp.concatenate(shifted_slot(j), axis=0)
        if q == 0:
            moved[slot_rows(0), :] = packed(halves(moved[slot_rows(0), :]), shifted_last())

    for it in range(ITERS):

        def part_steps(q):
            def begin():
                if it == 0:
                    forward_part(q)
                else:
                    shift_part(q)

            def end():
                if q == 0:
                    unpack(it)
                inverse_part(
                    it,
                    q,
                    lambda j: whiten(*slot_of(spec, first_f, j), *slot_of(tmpl.at[it], first_t.at[it], j)),
                    lambda: whiten(*halves(last_f[...]), *halves(last_t[it])),
                )

            steps = sum_steps(it, q, moved if it > 0 else spec)
            return [lambda: (begin(), steps[0]())] + steps[1:-1] + [lambda: (steps[-1](), end())]

        plan = [
            (SPACING[it] * q + STEP * k, q, step) for q in range(NQ) for k, step in enumerate(part_steps(q))
        ]
        for _, _, step in sorted(plan, key=lambda entry: entry[:2]):
            step()
        shifts = centroid(it)
        make_ramp(shifts)

    for q in range(NQ):
        inverse_part(ITERS, q, shifted_slot, shifted_last)
    inverse_x(ITERS, out_ref)
    by_z, by_x, by_y = shifts
    line = jnp.where(lane == 0, by_z, jnp.where(lane == 1, by_x, by_y))
    shift_ref[...] = line[:, 0:3]

    for copy in sends:
        copy.wait_send()

    def finish(q, carry):
        wait_sent(send_f, recv_f, fwd_send, fwd_recv, q, by_device)
        for n in range(ITERS + 1):
            wait_sent(send_i.at[n], recv_i.at[n], inv_send.at[n], inv_recv.at[n], q, by_part)
        return carry

    lax.fori_loop(0, NQ, finish, 0)
    for it in range(ITERS):

        def done(i, carry):
            d = (s + i) % SPACE
            pltpu.make_async_remote_copy(
                src_ref=stats_out.at[it],
                dst_ref=stats_in.at[it, s],
                send_sem=st_send.at[it, d],
                recv_sem=st_recv.at[it, s],
                device_id={"space": d},
                device_id_type=MESH,
            ).wait_send()
            return carry

        lax.fori_loop(1, SPACE, done, 0)


def body(volumes):
    consts = [jnp.asarray(table) for table in tables()]
    vmem = pl.BlockSpec(memory_space=pltpu.VMEM)
    hbm = pl.BlockSpec(memory_space=pltpu.HBM)
    dma = pltpu.SemaphoreType.DMA
    slots = SLOTS * 2 * Z
    corrected, shifts = pl.pallas_call(
        kernel,
        out_shape=(
            jax.ShapeDtypeStruct((SLABS, X, Y), F32),
            jax.ShapeDtypeStruct((1, 3), F32),
        ),
        in_specs=[hbm] * (1 + len(consts)),
        out_specs=(vmem, vmem),
        scratch_shapes=[
            pltpu.VMEM((SLABS, X, Y), F32),
            *[pltpu.VMEM(table.shape, BF16) for table in consts],
            pltpu.VMEM((ROWS, 128), F32),
            pltpu.VMEM((ROWS, 128), F32),
            pltpu.VMEM((slots, 128), F32),
            pltpu.VMEM((slots, 128), F32),
            pltpu.VMEM((2 * Z, 128), F32),
            pltpu.VMEM((2 * Z, 128), F32),
            pltpu.VMEM((ITERS, 2 * Z, 128), F32),
            pltpu.VMEM((ITERS, 2 * Z, 128), F32),
            pltpu.VMEM((ITERS, NQ, HALF, 128), F32),
            pltpu.VMEM((ITERS, NQ, HALF, 128), F32),
            pltpu.VMEM((ITERS, NQ, 7, UNIT, 128), F32),
            pltpu.VMEM((ITERS, NQ, 3, UNIT, 128), F32),
            pltpu.VMEM((ITERS, slots, 128), F32),
            pltpu.VMEM((ITERS + 1, ROWS, 128), F32),
            pltpu.VMEM((ITERS + 1, ROWS, 128), F32),
            pltpu.VMEM((SLABS, X, 128), F32),
            pltpu.VMEM((ITERS, 8, 128), F32),
            pltpu.VMEM((ITERS, SPACE, 8, 128), F32),
            pltpu.VMEM((2, Z, 128), F32),
            pltpu.VMEM((2, SLOTS, 8, 128), F32),
            dma((1 + len(consts),)),
            dma((NQ, SPACE)), dma((NQ, SPACE)),
            dma((ITERS + 1, NQ, SPACE)), dma((ITERS + 1, NQ, SPACE)),
            dma((ITERS, SPACE)), dma((ITERS, SPACE)),
            dma((ITERS, NQ)), dma((ITERS, NQ)),
            dma((ITERS, NQ, 7)), dma((ITERS, NQ, 7)),
            dma((ITERS, NQ, 7)), dma((ITERS, NQ, 7)),
            dma((ITERS, NQ)), dma((ITERS, NQ)),
        ],
        compiler_params=pltpu.CompilerParams(
            collective_id=0, has_side_effects=True, vmem_limit_bytes=56 * 2**20
        ),
        name="register",
    )(volumes[0], *consts)
    return corrected[None], shifts


def solution(mesh):
    in_specs = (P("tm", "space", None, None),)
    out_specs = (P("tm", "space", None, None), P("tm", None))
    return jax.shard_map(body, mesh=mesh, in_specs=in_specs, out_specs=out_specs, check_vma=False)
```

```python
import functools
import math

import jax
import jax.numpy as jnp
import ml_dtypes
import numpy as np
from jax import lax
from jax.experimental import pallas as pl
from jax.experimental.pallas import tpu as pltpu
from jax.sharding import PartitionSpec as P

X = 512
Y = 128
Z = 64
ITERS = 2
FRAMES = 16
NORM = 1.0 / (X * Y * Z)
SHARPNESS = 256.0
FLOOR = 0.05 * (X * Y * Z)

SPACE = 16
CHIPS = 8
SLABS = Z // SPACE
SLOTS = X // 2 // SPACE
ROWS = SPACE * SLOTS * 8
MSG = SLOTS * 8
NQ = 4
PART = MSG // NQ
HALF = SLOTS // NQ * Z
UNIT = HALF // CHIPS
GROUP = 4
GROUPS = SLOTS // NQ // GROUP
FIRST_SUMS = ((2, 1), (4, 1), (-3, -1), (-1, -1))
MERGED = (1, 3, -2)
MEANS = (-1, -3, 2, 1)
PASSED = ((1, -1), (3, -1), (-2, 1))
LAST_MEANS = (-1, 2, 4, -3)
REACHED = (1, -1, 2, -2, 3, -3)
SPACING = (3.0, 1.0)
STEP = 3.5
MESH = pl.DeviceIdType.MESH
F32 = jnp.float32
BF16 = jnp.bfloat16


def tables():
    def angles(n, rows, columns):
        return 2.0 * np.pi * ((rows[:, None] * columns[None, :]) % n) / n

    half = X // 2
    a = angles(X, np.arange(half), np.arange(X))
    sign = (-1.0) ** np.arange(X)
    cos_x, sin_x = np.cos(a), np.sin(a)
    im = -sin_x
    im[0] = sign
    forward_x = np.concatenate([cos_x, im])
    weight = np.full((X, 1), 2.0)
    weight[0] = weight[half] = 1.0
    inverse_x = (forward_x * weight).T

    a = angles(Y, np.arange(Y), np.arange(Y))
    c, s = np.cos(a), np.sin(a)
    forward_y = np.block([[c, -s], [s, c]])
    inverse_y = np.block([[c, s], [-s, c]])

    a = angles(Z, np.arange(Z), np.arange(Z))
    c, s = np.cos(a), np.sin(a)
    forward_z = np.block([[c, s], [-s, c]])
    inverse_z = np.block([[c, -s], [s, c]])
    order = np.arange(2 * Z).reshape(2, SPACE, SLABS).transpose(1, 0, 2).reshape(-1)
    forward_z = forward_z[:, order]
    inverse_z = inverse_z[order, :]

    slots = np.arange(X // 2).reshape(SPACE, 2, NQ // 2, SLOTS // NQ).transpose(1, 2, 0, 3).reshape(2, 1, -1)
    columns = slots + np.arange(2)[None, :, None] * (X // 2)

    def two(table):
        high = table.astype(np.float32).astype(ml_dtypes.bfloat16)
        return high, (table - high.astype(np.float64)).astype(np.float32).astype(ml_dtypes.bfloat16)

    def block(table):
        high, low = two(table)
        return np.concatenate(
            [np.concatenate([high, high], axis=1), np.concatenate([low, np.zeros_like(low)], axis=1)]
        )

    out = [
        np.concatenate(two(forward_x)),
        np.stack([np.concatenate(two(inverse_x[:, half.reshape(-1)])) for half in columns]),
        np.stack(two(forward_y)),
        np.stack(two(inverse_y)),
        block(forward_z),
        block(inverse_z),
    ]
    flips = [np.zeros((n, n), ml_dtypes.bfloat16) for n in (Z, Y)]
    for flip in flips:
        flip[np.arange(len(flip)), -np.arange(len(flip))] = 1.0
    return out + flips


def split(value):
    high = value.astype(BF16)
    return high, (value - high.astype(F32)).astype(BF16)


def dot(a, b):
    return jnp.dot(a, b, preferred_element_type=F32)


def x_dot(table, data):
    n = table.shape[0] // 2
    data_high, data_low = split(data)
    both = dot(table, data_high)
    return both[:n] + (both[n:] + dot(table[:n], data_low))


def z_dot(table, data):
    n = table.shape[0] // 2
    both = dot(table, jnp.concatenate(split(data), axis=0))
    return both[:n] + both[n:]


def dot_y(data, table):
    n = data.shape[0]
    data_high, data_low = split(data)
    both = dot(jnp.concatenate([data_high, data_low], axis=0), table[0])
    return both[:n] + (both[n:] + dot(data_high, table[1]))


def rows_of(start, count):
    return pl.ds(start if isinstance(start, int) else pl.multiple_of(start, 8), count)


def signed(index, n):
    wrapped = jnp.where(index < n // 2, index, index - n)
    return jnp.where(index == n // 2, 0, wrapped).astype(F32)


def kernel(
    v_hbm, fx_hbm, ix_hbm, fy_hbm, iy_hbm, fz_hbm, iz_hbm, flip_z_hbm, flip_y_hbm,
    out_hbm, shift_ref,
    v_ref, fx, ix, fy, iy, fz, iz, flip_z, flip_y,
    out_ref, out_sem, send_f, recv_f, spec, moved, first_f, last_f, first_t, last_t, other, pair,
    sums_in, sums_out, tmpl,
    send_i, recv_i, scores, stats_out, stats_in, ramp_zy, ramp_x,
    load_sem, fwd_send, fwd_recv, inv_send, inv_recv, st_send, st_recv,
    oc_send, oc_recv, sum_send, sum_recv, mean_send, mean_recv, go_send, go_recv,
):
    s = lax.axis_index("space")
    t = lax.axis_index("tm")
    core = t % 2
    chip = t // 2
    mate = chip * 2 + 1 - core

    loads = [
        pltpu.make_async_copy(source, target, load_sem.at[i])
        for i, (source, target) in enumerate(
            [
                (fx_hbm, fx), (v_hbm, v_ref), (fz_hbm, fz), (fy_hbm, fy), (iy_hbm, iy),
                (iz_hbm, iz), (flip_z_hbm, flip_z), (flip_y_hbm, flip_y), (ix_hbm, ix),
            ]
        )
    ]
    for copy in loads:
        copy.start()

    barrier = pltpu.get_barrier_semaphore()

    def greet(i, carry):
        pl.semaphore_signal(barrier, inc=1, device_id={"space": (s + i) % SPACE}, device_id_type=MESH)
        return carry

    lax.fori_loop(1, SPACE, greet, 0)
    for offset in REACHED:
        member = ((chip + CHIPS + offset) % CHIPS) * 2 + core
        pl.semaphore_signal(barrier, inc=1, device_id={"tm": member}, device_id_type=MESH)
    pl.semaphore_signal(barrier, inc=1, device_id={"tm": mate}, device_id_type=MESH)

    row = lax.broadcasted_iota(jnp.int32, (2 * Z, 128), 0)
    first_part = (row // SLABS) % 2 == 0

    def to_space(source, start, target, target_start, send_sem, recv_sem, device, count):
        return pltpu.make_async_remote_copy(
            src_ref=source.at[rows_of(start, count)],
            dst_ref=target.at[rows_of(target_start, count)],
            send_sem=send_sem,
            recv_sem=recv_sem,
            device_id={"space": device},
            device_id_type=MESH,
        )

    for copy in loads[:2]:
        copy.wait()

    for z in range(0, SLABS, 2):
        data = jnp.concatenate([v_ref[z], v_ref[z + 1]], axis=1)
        result = x_dot(fx[...], data)
        for i in range(2):
            for part in range(2):
                send_f[pl.ds(part * SLABS + z + i, X // 2, stride=8), :] = result[
                    part * (X // 2) : (part + 1) * (X // 2), i * 128 : (i + 1) * 128
                ]

    pl.semaphore_wait(barrier, SPACE + len(REACHED))

    def by_device(device, q):
        return device * MSG + q * PART

    def by_part(device, q):
        return (q * SPACE + device) * PART

    def exchange_part(source, target, send_sem, recv_sem, q, place):
        def one(i, carry):
            d = (s + i) % SPACE
            to_space(
                source, by_device(d, q), target, place(s, q), send_sem.at[q, d], recv_sem.at[q, s], d, PART
            ).start()
            return carry

        lax.fori_loop(1, SPACE, one, 0)
        target[rows_of(place(s, q), PART), :] = source[rows_of(by_device(s, q), PART), :]

    def wait_part(source, target, send_sem, recv_sem, q, place):
        def one(i, carry):
            d = (s + i) % SPACE
            to_space(
                source, by_device(d, q), target, place(d, q), send_sem.at[q, d], recv_sem.at[q, d], d, PART
            ).wait_recv()
            return carry

        lax.fori_loop(1, SPACE, one, 0)

    def wait_sent(source, target, send_sem, recv_sem, q, place):
        def one(i, carry):
            d = (s + i) % SPACE
            to_space(
                source, by_device(d, q), target, place(s, q), send_sem.at[q, d], recv_sem.at[q, s], d, PART
            ).wait_send()
            return carry

        lax.fori_loop(1, SPACE, one, 0)

    def send_all(q, carry):
        exchange_part(send_f, recv_f, fwd_send, fwd_recv, q, by_device)
        return carry

    lax.fori_loop(0, NQ, send_all, 0)
    for copy in loads[2:]:
        copy.wait()

    def load_slot(j):
        return jnp.concatenate([recv_f[rows_of(d * MSG + j * 8, 8), :] for d in range(SPACE)], axis=0)

    def complex_rows(value):
        return jnp.concatenate([value[:Z], value[Z:]], axis=1)

    def part_rows(value):
        return jnp.concatenate([value[:, :128], value[:, 128:]], axis=0)

    def spectrum_of(slots):
        zed = z_dot(fz[...], jnp.concatenate(slots, axis=1))
        lines = [complex_rows(zed[:, i * 128 : (i + 1) * 128]) for i in range(len(slots))]
        freq = dot_y(jnp.concatenate(lines, axis=0), fy)
        return [part_rows(freq[i * Z : (i + 1) * Z]) for i in range(len(slots))]

    def slot_rows(j):
        return rows_of(j * 2 * Z, 2 * Z)

    def groups(q):
        return [[GROUP * i + k for k in range(GROUP)] for i in range(q * GROUPS, (q + 1) * GROUPS)]

    owner = jnp.where(s == 0, 1.0, 0.0)

    def forward_part(q):
        wait_part(send_f, recv_f, fwd_send, fwd_recv, q, by_device)
        for group in groups(q):
            for j, value in zip(group, spectrum_of([load_slot(j) for j in group])):
                spec[slot_rows(j), :] = value
        if q == 0:
            slot = load_slot(0)
            keep = jnp.where(first_part, 1.0, 1.0 - owner)
            rolled = jnp.concatenate([slot[SLABS:], slot[:SLABS]], axis=0)
            first_f[...], last_f[...] = spectrum_of(
                [slot * keep, rolled * jnp.where(first_part, owner, 0.0)]
            )

    sends = []

    def to_tm(source, target, send_sem, recv_sem, device):
        return pltpu.make_async_remote_copy(
            src_ref=source,
            dst_ref=target,
            send_sem=send_sem,
            recv_sem=recv_sem,
            device_id={"tm": device},
            device_id_type=MESH,
        )

    def start(copy):
        copy.start()
        sends.append(copy)

    def half_rows(q, c):
        return rows_of((2 * q + c) * HALF, HALF)

    def sum_steps(it, q, source):
        side = 1 - 2 * (q % 2)

        def pair_unit(i):
            return pair.at[it, q, rows_of((i % CHIPS) * UNIT, UNIT)]

        def mean_unit(i):
            return tmpl.at[it, rows_of((2 * q + core) * HALF + (i % CHIPS) * UNIT, UNIT)]

        def swap():
            return to_tm(source.at[half_rows(q, 1 - core)], other.at[it, q], oc_send.at[it, q], oc_recv.at[it, q], mate)

        def chip_at(offset):
            return ((chip + CHIPS + side * offset) % CHIPS) * 2 + core

        def sum_copy(outgoing, k, offset):
            return to_tm(outgoing, sums_in.at[it, q, k], sum_send.at[it, q, k], sum_recv.at[it, q, k], chip_at(offset))

        def mean_copy(i, k, offset):
            ref = mean_unit(chip + CHIPS + side * i)
            return to_tm(ref, ref, mean_send.at[it, q, k], mean_recv.at[it, q, k], chip_at(offset))

        def to_mate(c):
            ref = tmpl.at[it, half_rows(q, c)]
            return to_tm(ref, ref, go_send.at[it, q], go_recv.at[it, q], mate)

        def step_swap():
            start(swap())

        def step_pair():
            swap().wait_recv()
            pair[it, q] = source[half_rows(q, core), :] + other[it, q]
            for k, (i, offset) in enumerate(FIRST_SUMS):
                start(sum_copy(pair_unit(chip + CHIPS + side * i), k, offset))

        def step_merge():
            for k, i in enumerate(MERGED):
                sum_copy(sums_out.at[it, q, k], k, i).wait_recv()
                sums_out[it, q, k] = pair_unit(chip + CHIPS + side * i)[...] + sums_in[it, q, k]
                start(sum_copy(sums_out.at[it, q, k], len(FIRST_SUMS) + k, i))

        def step_mean():
            total = pair_unit(chip)[...]
            for k in range(len(MERGED), CHIPS - 1):
                sum_copy(sums_in.at[it, q, k], k, 1).wait_recv()
                total = total + sums_in[it, q, k]
            tmpl[it, rows_of((2 * q + core) * HALF + chip * UNIT, UNIT), :] = total * (1.0 / FRAMES)
            for k, offset in enumerate(MEANS):
                start(mean_copy(0, k, offset))

        def step_pass():
            for k, (i, offset) in enumerate(PASSED):
                mean_copy(i, k, 1).wait_recv()
                start(mean_copy(i, len(MEANS) + k, offset))

        def step_share():
            for k, i in enumerate(LAST_MEANS):
                mean_copy(i, len(PASSED) + k, 1).wait_recv()
            start(to_mate(core))

        def step_end():
            to_mate(1 - core).wait_recv()

        steps = [step_swap, step_pair, step_merge, step_mean, step_pass, step_share, step_end]
        return [step for step in steps if (MERGED or step is not step_merge) and (PASSED or step is not step_pass)]

    def whiten(f_re, f_im, t_re, t_im):
        p_re = f_re * t_re + f_im * t_im
        p_im = f_im * t_re - f_re * t_im
        scale = lax.rsqrt(jnp.maximum(p_re * p_re + p_im * p_im, FLOOR * FLOOR))
        return p_re * scale, p_im * scale

    def halves(value):
        return value[:Z], value[Z:]

    def slot_of(ref, first, j):
        return halves(first[...] if j == 0 else ref[slot_rows(j), :])

    def packed(first, last):
        (f_re, f_im), (l_re, l_im) = first, last
        return jnp.concatenate([f_re - l_im, f_im + l_re], axis=0)

    def flipped(value):
        high, low = split(value)
        value = dot(flip_z[...], high) + dot(flip_z[...], low)
        high, low = split(part_rows(value))
        return halves(dot(high, flip_y[...]) + dot(low, flip_y[...]))

    def unpack(it):
        value = tmpl[it, slot_rows(0), :]
        re, im = halves(value)
        flip_re, flip_im = flipped(complex_rows(value))
        half = 0.5 * owner
        first_t[it] = jnp.concatenate([re - half * (re - flip_re), im - half * (im + flip_im)], axis=0)
        last_t[it] = jnp.concatenate([half * (im + flip_im), half * (flip_re - re)], axis=0)

    def back(values):
        lines = [jnp.concatenate([re, im], axis=1) for re, im in values]
        lines = dot_y(jnp.concatenate(lines, axis=0), iy)
        planes = [part_rows(lines[i * Z : (i + 1) * Z]) for i in range(len(values))]
        return z_dot(iz[...], jnp.concatenate(planes, axis=1))

    def inverse_part(n, q, slot_values, last_values):
        if q == 0:
            last = back([last_values()])
            last = jnp.concatenate([last[2 * Z - SLABS :], last[: 2 * Z - SLABS]], axis=0)

        for group in groups(q):
            planes = back([slot_values(j) for j in group])
            for k, j in enumerate(group):
                value = planes[:, k * 128 : (k + 1) * 128]
                if j == 0:
                    keep = jnp.where(first_part, 1.0, 1.0 - owner)
                    value = value * keep + last * (1.0 - keep)
                for d in range(SPACE):
                    send_i[n, rows_of(d * MSG + j * 8, 8), :] = value[8 * d : 8 * d + 8]
        exchange_part(send_i.at[n], recv_i.at[n], inv_send.at[n], inv_recv.at[n], q, by_part)

    def store_planes(z):
        planes = pl.ds(z, 2)
        return pltpu.make_async_copy(out_ref.at[planes], out_hbm.at[planes], out_sem.at[z // 2])

    def inverse_x(n, target):
        count = ROWS // 16

        def wait_one(q, carry):
            wait_part(send_i.at[n], recv_i.at[n], inv_send.at[n], inv_recv.at[n], q, by_part)
            return carry

        for half in range(2):
            lax.fori_loop(half * (NQ // 2), (half + 1) * (NQ // 2), wait_one, 0)
            for z in range(0, SLABS, 2):
                columns = []
                for i in range(2):
                    parts = [
                        recv_i[n, pl.ds(half * count * 8 + part * SLABS + z + i, count, stride=8), :]
                        for part in range(2)
                    ]
                    columns.append(jnp.concatenate(parts, axis=0))
                value = x_dot(ix[half], jnp.concatenate(columns, axis=1))
                for i in range(2):
                    plane = value[:, i * 128 : (i + 1) * 128]
                    target[z + i] = plane if half == 0 else target[z + i] + plane
                if half == 1 and n == ITERS:
                    store_planes(z).start()

    lane = lax.broadcasted_iota(jnp.int32, (1, 128), 1)

    def centroid(it):
        top = jnp.full((8, 128), -jnp.inf, F32)
        inverse_x(it, scores)
        for z in range(SLABS):
            top = jnp.maximum(top, jnp.max(scores[z].reshape(X // 8, 8, 128), axis=0))
        top = top * (SHARPNESS * NORM)
        top = jnp.max(jnp.max(top, axis=0, keepdims=True), axis=1, keepdims=True)
        step = 128
        x_row = lax.broadcasted_iota(jnp.int32, (step, 128), 0)
        zero = jnp.zeros((8, 128), F32)

        def weigh(i, carry):
            total, by_z, by_x = carry
            z, x = i // (X // step), (i % (X // step)) * step
            weights = jnp.exp(scores[z, rows_of(x, step), :] * (SHARPNESS * NORM) - top)
            x_at = ((x + x_row + X // 2) % X - X // 2).astype(F32)
            z_at = ((s * SLABS + z + Z // 2) % Z - Z // 2).astype(F32)
            here = jnp.sum(weights.reshape(step // 8, 8, 128), axis=0)
            by_x = by_x + jnp.sum((weights * x_at).reshape(step // 8, 8, 128), axis=0)
            return total + here, by_z + here * z_at, by_x

        total, by_z, by_x = lax.fori_loop(0, SLABS * X // step, weigh, (zero, zero, zero))
        y_at = ((lane + Y // 2) % Y - Y // 2).astype(F32)
        sums = [jnp.sum(value, axis=0, keepdims=True) for value in (total, by_z, by_x)]
        rows = [jnp.broadcast_to(top, (1, 128))] + sums + [sums[0] * y_at, jnp.zeros((3, 128), F32)]
        tile = jnp.concatenate(rows, axis=0)
        stats_out[it] = tile
        stats_in[it, s] = tile

        def stat(i, target, sender):
            d = (s + i) % SPACE
            return pltpu.make_async_remote_copy(
                src_ref=stats_out.at[it],
                dst_ref=stats_in.at[it, s if sender else d],
                send_sem=st_send.at[it, d],
                recv_sem=st_recv.at[it, s if sender else d],
                device_id={"space": d},
                device_id_type=MESH,
            )

        def send(i, carry):
            stat(i, s, True).start()
            return carry

        def receive(i, carry):
            stat(i, s, False).wait_recv()
            return carry

        lax.fori_loop(1, SPACE, send, 0)
        lax.fori_loop(1, SPACE, receive, 0)
        every = stats_in[it]
        tops = every[:, 0:1, :]
        scale = jnp.exp(tops - jnp.max(tops, axis=0, keepdims=True))
        sums = jnp.sum(jnp.sum(every * scale, axis=0), axis=1, keepdims=True)
        return [sums[i : i + 1] / sums[1:2] for i in (2, 3, 4)]

    def make_ramp(shifts):
        by_z, by_x, by_y = shifts
        kz = lax.broadcasted_iota(jnp.int32, (Z, 128), 0)
        ky = lax.broadcasted_iota(jnp.int32, (Z, 128), 1)
        phase = (2.0 * math.pi) * (signed(kz, Z) * (by_z / Z) + signed(ky, Y) * (by_y / Y))
        ramp_zy[0] = jnp.cos(phase)
        ramp_zy[1] = jnp.sin(phase)
        kx = s * SLOTS + lax.broadcasted_iota(jnp.int32, (SLOTS, 128), 0)
        phase = (2.0 * math.pi) * (kx.astype(F32) * (by_x / X))
        cos_x, sin_x = jnp.cos(phase), jnp.sin(phase)
        for j in range(SLOTS):
            ramp_x[0, j] = jnp.broadcast_to(cos_x[j : j + 1], (8, 128))
            ramp_x[1, j] = jnp.broadcast_to(sin_x[j : j + 1], (8, 128))

    def shifted_slot(j):
        cos_x = jnp.concatenate([ramp_x[0, j]] * (Z // 8), axis=0)
        sin_x = jnp.concatenate([ramp_x[1, j]] * (Z // 8), axis=0)
        cosine = ramp_zy[0] * cos_x - ramp_zy[1] * sin_x
        sine = ramp_zy[1] * cos_x + ramp_zy[0] * sin_x
        f_re, f_im = slot_of(spec, first_f, j)
        return f_re * cosine - f_im * sine, f_re * sine + f_im * cosine

    def shifted_last():
        f_re, f_im = halves(last_f[...])
        return f_re * ramp_zy[0] - f_im * ramp_zy[1], f_re * ramp_zy[1] + f_im * ramp_zy[0]

    def shift_part(q):
        for group in groups(q):
            for j in group:
                moved[slot_rows(j), :] = jnp.concatenate(shifted_slot(j), axis=0)
        if q == 0:
            moved[slot_rows(0), :] = packed(halves(moved[slot_rows(0), :]), shifted_last())

    for it in range(ITERS):

        def part_steps(q):
            def begin():
                if it == 0:
                    forward_part(q)
                else:
                    shift_part(q)

            def end():
                if q == 0:
                    unpack(it)
                inverse_part(
                    it,
                    q,
                    lambda j: whiten(*slot_of(spec, first_f, j), *slot_of(tmpl.at[it], first_t.at[it], j)),
                    lambda: whiten(*halves(last_f[...]), *halves(last_t[it])),
                )

            steps = sum_steps(it, q, moved if it > 0 else spec)
            return [lambda: (begin(), steps[0]())] + steps[1:-1] + [lambda: (steps[-1](), end())]

        plan = [
            (SPACING[it] * q + STEP * k, q, step) for q in range(NQ) for k, step in enumerate(part_steps(q))
        ]
        for _, _, step in sorted(plan, key=lambda entry: entry[:2]):
            step()
        shifts = centroid(it)
        make_ramp(shifts)

    for q in range(NQ):
        inverse_part(ITERS, q, shifted_slot, shifted_last)
    inverse_x(ITERS, out_ref)
    by_z, by_x, by_y = shifts
    line = jnp.where(lane == 0, by_z, jnp.where(lane == 1, by_x, by_y))
    shift_ref[...] = line[:, 0:3]

    for copy in sends:
        copy.wait_send()
    for z in range(0, SLABS, 2):
        store_planes(z).wait()

    def finish(q, carry):
        wait_sent(send_f, recv_f, fwd_send, fwd_recv, q, by_device)
        for n in range(ITERS + 1):
            wait_sent(send_i.at[n], recv_i.at[n], inv_send.at[n], inv_recv.at[n], q, by_part)
        return carry

    lax.fori_loop(0, NQ, finish, 0)
    for it in range(ITERS):

        def done(i, carry):
            d = (s + i) % SPACE
            pltpu.make_async_remote_copy(
                src_ref=stats_out.at[it],
                dst_ref=stats_in.at[it, s],
                send_sem=st_send.at[it, d],
                recv_sem=st_recv.at[it, s],
                device_id={"space": d},
                device_id_type=MESH,
            ).wait_send()
            return carry

        lax.fori_loop(1, SPACE, done, 0)


def body(volumes):
    consts = [jnp.asarray(table) for table in tables()]
    vmem = pl.BlockSpec(memory_space=pltpu.VMEM)
    hbm = pl.BlockSpec(memory_space=pltpu.HBM)
    dma = pltpu.SemaphoreType.DMA
    slots = SLOTS * 2 * Z
    corrected, shifts = pl.pallas_call(
        kernel,
        out_shape=(
            jax.ShapeDtypeStruct((SLABS, X, Y), F32),
            jax.ShapeDtypeStruct((1, 3), F32),
        ),
        in_specs=[hbm] * (1 + len(consts)),
        out_specs=(hbm, vmem),
        scratch_shapes=[
            pltpu.VMEM((SLABS, X, Y), F32),
            *[pltpu.VMEM(table.shape, BF16) for table in consts],
            pltpu.VMEM((SLABS, X, Y), F32),
            dma((SLABS // 2,)),
            pltpu.VMEM((ROWS, 128), F32),
            pltpu.VMEM((ROWS, 128), F32),
            pltpu.VMEM((slots, 128), F32),
            pltpu.VMEM((slots, 128), F32),
            pltpu.VMEM((2 * Z, 128), F32),
            pltpu.VMEM((2 * Z, 128), F32),
            pltpu.VMEM((ITERS, 2 * Z, 128), F32),
            pltpu.VMEM((ITERS, 2 * Z, 128), F32),
            pltpu.VMEM((ITERS, NQ, HALF, 128), F32),
            pltpu.VMEM((ITERS, NQ, HALF, 128), F32),
            pltpu.VMEM((ITERS, NQ, 7, UNIT, 128), F32),
            pltpu.VMEM((ITERS, NQ, 3, UNIT, 128), F32),
            pltpu.VMEM((ITERS, slots, 128), F32),
            pltpu.VMEM((ITERS + 1, ROWS, 128), F32),
            pltpu.VMEM((ITERS + 1, ROWS, 128), F32),
            pltpu.VMEM((SLABS, X, 128), F32),
            pltpu.VMEM((ITERS, 8, 128), F32),
            pltpu.VMEM((ITERS, SPACE, 8, 128), F32),
            pltpu.VMEM((2, Z, 128), F32),
            pltpu.VMEM((2, SLOTS, 8, 128), F32),
            dma((1 + len(consts),)),
            dma((NQ, SPACE)), dma((NQ, SPACE)),
            dma((ITERS + 1, NQ, SPACE)), dma((ITERS + 1, NQ, SPACE)),
            dma((ITERS, SPACE)), dma((ITERS, SPACE)),
            dma((ITERS, NQ)), dma((ITERS, NQ)),
            dma((ITERS, NQ, 7)), dma((ITERS, NQ, 7)),
            dma((ITERS, NQ, 7)), dma((ITERS, NQ, 7)),
            dma((ITERS, NQ)), dma((ITERS, NQ)),
        ],
        compiler_params=pltpu.CompilerParams(
            collective_id=0, has_side_effects=True, vmem_limit_bytes=56 * 2**20
        ),
        name="register",
    )(volumes[0], *consts)
    return corrected[None] * NORM, shifts


def solution(mesh):
    in_specs = (P("tm", "space", None, None),)
    out_specs = (P("tm", "space", None, None), P("tm", None))
    return jax.shard_map(body, mesh=mesh, in_specs=in_specs, out_specs=out_specs, check_vma=False)
```

```python
import functools
import math

import jax
import jax.numpy as jnp
import ml_dtypes
import numpy as np
from jax import lax
from jax.experimental import pallas as pl
from jax.experimental.pallas import tpu as pltpu
from jax.sharding import PartitionSpec as P

X = 512
Y = 128
Z = 64
ITERS = 2
FRAMES = 16
NORM = 1.0 / (X * Y * Z)
SHARPNESS = 256.0
FLOOR = 0.05 * (X * Y * Z)

SPACE = 16
CHIPS = 8
SLABS = Z // SPACE
SLOTS = X // 2 // SPACE
ROWS = SPACE * SLOTS * 8
MSG = SLOTS * 8
NQ = 4
PART = MSG // NQ
HALF = SLOTS // NQ * Z
UNIT = HALF // CHIPS
GROUP = 4
GROUPS = SLOTS // NQ // GROUP
FIRST_SUMS = ((2, 1), (4, 1), (-3, -1), (-1, -1))
MERGED = (1, 3, -2)
MEANS = (-1, -3, 2, 1)
PASSED = ((1, -1), (3, -1), (-2, 1))
LAST_MEANS = (-1, 2, 4, -3)
REACHED = (1, -1, 2, -2, 3, -3)
SPACING = (3.0, 1.0)
STEP = 3.5
MESH = pl.DeviceIdType.MESH
F32 = jnp.float32
BF16 = jnp.bfloat16


def tables():
    def angles(n, rows, columns):
        return 2.0 * np.pi * ((rows[:, None] * columns[None, :]) % n) / n

    half = X // 2
    a = angles(X, np.arange(half), np.arange(X))
    sign = (-1.0) ** np.arange(X)
    cos_x, sin_x = np.cos(a), np.sin(a)
    im = -sin_x
    im[0] = sign
    forward_x = np.concatenate([cos_x, im])
    weight = np.full((X, 1), 2.0)
    weight[0] = weight[half] = 1.0
    inverse_x = (forward_x * weight).T

    a = angles(Y, np.arange(Y), np.arange(Y))
    c, s = np.cos(a), np.sin(a)
    forward_y = np.block([[c, -s], [s, c]])
    inverse_y = np.block([[c, s], [-s, c]])

    a = angles(Z, np.arange(Z), np.arange(Z))
    c, s = np.cos(a), np.sin(a)
    forward_z = np.block([[c, s], [-s, c]])
    inverse_z = np.block([[c, -s], [s, c]])
    order = np.arange(2 * Z).reshape(2, SPACE, SLABS).transpose(1, 0, 2).reshape(-1)
    forward_z = forward_z[:, order]
    inverse_z = inverse_z[order, :]

    slots = np.arange(X // 2).reshape(SPACE, 2, NQ // 2, SLOTS // NQ).transpose(1, 2, 0, 3).reshape(2, 1, -1)
    columns = slots + np.arange(2)[None, :, None] * (X // 2)

    def two(table):
        high = table.astype(np.float32).astype(ml_dtypes.bfloat16)
        return high, (table - high.astype(np.float64)).astype(np.float32).astype(ml_dtypes.bfloat16)

    def block(table):
        high, low = two(table)
        return np.concatenate(
            [np.concatenate([high, high], axis=1), np.concatenate([low, np.zeros_like(low)], axis=1)]
        )

    out = [
        np.concatenate(two(forward_x)),
        np.stack([np.concatenate(two(inverse_x[:, half.reshape(-1)])) for half in columns]),
        np.stack(two(forward_y)),
        np.stack(two(inverse_y)),
        block(forward_z),
        block(inverse_z),
    ]
    flips = [np.zeros((n, n), ml_dtypes.bfloat16) for n in (Z, Y)]
    for flip in flips:
        flip[np.arange(len(flip)), -np.arange(len(flip))] = 1.0
    return out + flips


def split(value):
    high = value.astype(BF16)
    return high, (value - high.astype(F32)).astype(BF16)


def dot(a, b):
    return jnp.dot(a, b, preferred_element_type=F32)


def x_dot(table, data):
    n = table.shape[0] // 2
    data_high, data_low = split(data)
    both = dot(table, data_high)
    return both[:n] + (both[n:] + dot(table[:n], data_low))


def z_dot(table, data):
    n = table.shape[0] // 2
    both = dot(table, jnp.concatenate(split(data), axis=0))
    return both[:n] + both[n:]


def dot_y(data, table):
    n = data.shape[0]
    data_high, data_low = split(data)
    both = dot(jnp.concatenate([data_high, data_low], axis=0), table[0])
    return both[:n] + (both[n:] + dot(data_high, table[1]))


def rows_of(start, count):
    return pl.ds(start if isinstance(start, int) else pl.multiple_of(start, 8), count)


def signed(index, n):
    wrapped = jnp.where(index < n // 2, index, index - n)
    return jnp.where(index == n // 2, 0, wrapped).astype(F32)


def kernel(
    v_hbm, fx_hbm, ix_hbm, fy_hbm, iy_hbm, fz_hbm, iz_hbm, flip_z_hbm, flip_y_hbm,
    out_hbm, shift_ref,
    v_ref, fx, ix, fy, iy, fz, iz, flip_z, flip_y,
    out_ref, out_sem, send_f, recv_f, spec, moved, first_f, last_f, first_t, last_t, other, pair,
    sums_in, sums_out, tmpl,
    send_i, recv_i, scores, stats_out, stats_in, ramp_zy, ramp_x,
    load_sem, fwd_send, fwd_recv, inv_send, inv_recv, st_send, st_recv,
    oc_send, oc_recv, sum_send, sum_recv, mean_send, mean_recv, go_send, go_recv,
):
    s = lax.axis_index("space")
    t = lax.axis_index("tm")
    core = t % 2
    chip = t // 2
    mate = chip * 2 + 1 - core

    loads = [
        pltpu.make_async_copy(source, target, load_sem.at[i])
        for i, (source, target) in enumerate(
            [
                (fx_hbm, fx), (v_hbm, v_ref), (fz_hbm, fz), (fy_hbm, fy), (iy_hbm, iy),
                (iz_hbm, iz), (flip_z_hbm, flip_z), (flip_y_hbm, flip_y), (ix_hbm, ix),
            ]
        )
    ]
    for copy in loads:
        copy.start()

    barrier = pltpu.get_barrier_semaphore()

    def greet(i, carry):
        pl.semaphore_signal(barrier, inc=1, device_id={"space": (s + i) % SPACE}, device_id_type=MESH)
        return carry

    lax.fori_loop(1, SPACE, greet, 0)
    for offset in REACHED:
        member = ((chip + CHIPS + offset) % CHIPS) * 2 + core
        pl.semaphore_signal(barrier, inc=1, device_id={"tm": member}, device_id_type=MESH)
    pl.semaphore_signal(barrier, inc=1, device_id={"tm": mate}, device_id_type=MESH)

    row = lax.broadcasted_iota(jnp.int32, (2 * Z, 128), 0)
    first_part = (row // SLABS) % 2 == 0

    def to_space(source, start, target, target_start, send_sem, recv_sem, device, count):
        return pltpu.make_async_remote_copy(
            src_ref=source.at[rows_of(start, count)],
            dst_ref=target.at[rows_of(target_start, count)],
            send_sem=send_sem,
            recv_sem=recv_sem,
            device_id={"space": device},
            device_id_type=MESH,
        )

    for copy in loads[:2]:
        copy.wait()

    for z in range(0, SLABS, 2):
        data = jnp.concatenate([v_ref[z], v_ref[z + 1]], axis=1)
        result = x_dot(fx[...], data)
        for i in range(2):
            for part in range(2):
                send_f[pl.ds(part * SLABS + z + i, X // 2, stride=8), :] = result[
                    part * (X // 2) : (part + 1) * (X // 2), i * 128 : (i + 1) * 128
                ]

    pl.semaphore_wait(barrier, SPACE + len(REACHED))

    def by_device(device, q):
        return device * MSG + q * PART

    def by_part(device, q):
        return (q * SPACE + device) * PART

    def exchange_part(source, target, send_sem, recv_sem, q, place):
        def one(i, carry):
            d = (s + i) % SPACE
            to_space(
                source, by_device(d, q), target, place(s, q), send_sem.at[q, d], recv_sem.at[q, s], d, PART
            ).start()
            return carry

        lax.fori_loop(1, SPACE, one, 0)
        target[rows_of(place(s, q), PART), :] = source[rows_of(by_device(s, q), PART), :]

    def wait_part(source, target, send_sem, recv_sem, q, place):
        def one(i, carry):
            d = (s + i) % SPACE
            to_space(
                source, by_device(d, q), target, place(d, q), send_sem.at[q, d], recv_sem.at[q, d], d, PART
            ).wait_recv()
            return carry

        lax.fori_loop(1, SPACE, one, 0)

    def wait_sent(source, target, send_sem, recv_sem, q, place):
        def one(i, carry):
            d = (s + i) % SPACE
            to_space(
                source, by_device(d, q), target, place(s, q), send_sem.at[q, d], recv_sem.at[q, s], d, PART
            ).wait_send()
            return carry

        lax.fori_loop(1, SPACE, one, 0)

    def send_all(q, carry):
        exchange_part(send_f, recv_f, fwd_send, fwd_recv, q, by_device)
        return carry

    lax.fori_loop(0, NQ, send_all, 0)
    for copy in loads[2:]:
        copy.wait()

    def load_slot(j):
        return jnp.concatenate([recv_f[rows_of(d * MSG + j * 8, 8), :] for d in range(SPACE)], axis=0)

    def complex_rows(value):
        return jnp.concatenate([value[:Z], value[Z:]], axis=1)

    def part_rows(value):
        return jnp.concatenate([value[:, :128], value[:, 128:]], axis=0)

    def spectrum_of(slots):
        zed = z_dot(fz[...], jnp.concatenate(slots, axis=1))
        lines = [complex_rows(zed[:, i * 128 : (i + 1) * 128]) for i in range(len(slots))]
        freq = dot_y(jnp.concatenate(lines, axis=0), fy)
        return [part_rows(freq[i * Z : (i + 1) * Z]) for i in range(len(slots))]

    def slot_rows(j):
        return rows_of(j * 2 * Z, 2 * Z)

    def groups(q):
        return [[GROUP * i + k for k in range(GROUP)] for i in range(q * GROUPS, (q + 1) * GROUPS)]

    owner = jnp.where(s == 0, 1.0, 0.0)

    def forward_part(q):
        wait_part(send_f, recv_f, fwd_send, fwd_recv, q, by_device)
        for group in groups(q):
            for j, value in zip(group, spectrum_of([load_slot(j) for j in group])):
                spec[slot_rows(j), :] = value
        if q == 0:
            slot = load_slot(0)
            keep = jnp.where(first_part, 1.0, 1.0 - owner)
            rolled = jnp.concatenate([slot[SLABS:], slot[:SLABS]], axis=0)
            first_f[...], last_f[...] = spectrum_of(
                [slot * keep, rolled * jnp.where(first_part, owner, 0.0)]
            )

    sends = []

    def to_tm(source, target, send_sem, recv_sem, device):
        return pltpu.make_async_remote_copy(
            src_ref=source,
            dst_ref=target,
            send_sem=send_sem,
            recv_sem=recv_sem,
            device_id={"tm": device},
            device_id_type=MESH,
        )

    def start(copy):
        copy.start()
        sends.append(copy)

    def half_rows(q, c):
        return rows_of((2 * q + c) * HALF, HALF)

    def sum_steps(it, q, source):
        side = 1 - 2 * (q % 2)

        def pair_unit(i):
            return pair.at[it, q, rows_of((i % CHIPS) * UNIT, UNIT)]

        def mean_unit(i):
            return tmpl.at[it, rows_of((2 * q + core) * HALF + (i % CHIPS) * UNIT, UNIT)]

        def swap():
            return to_tm(source.at[half_rows(q, 1 - core)], other.at[it, q], oc_send.at[it, q], oc_recv.at[it, q], mate)

        def chip_at(offset):
            return ((chip + CHIPS + side * offset) % CHIPS) * 2 + core

        def sum_copy(outgoing, k, offset):
            return to_tm(outgoing, sums_in.at[it, q, k], sum_send.at[it, q, k], sum_recv.at[it, q, k], chip_at(offset))

        def mean_copy(i, k, offset):
            ref = mean_unit(chip + CHIPS + side * i)
            return to_tm(ref, ref, mean_send.at[it, q, k], mean_recv.at[it, q, k], chip_at(offset))

        def to_mate(c):
            ref = tmpl.at[it, half_rows(q, c)]
            return to_tm(ref, ref, go_send.at[it, q], go_recv.at[it, q], mate)

        def step_swap():
            start(swap())

        def step_pair():
            swap().wait_recv()
            pair[it, q] = source[half_rows(q, core), :] + other[it, q]
            for k, (i, offset) in enumerate(FIRST_SUMS):
                start(sum_copy(pair_unit(chip + CHIPS + side * i), k, offset))

        def step_merge():
            for k, i in enumerate(MERGED):
                sum_copy(sums_out.at[it, q, k], k, i).wait_recv()
                sums_out[it, q, k] = pair_unit(chip + CHIPS + side * i)[...] + sums_in[it, q, k]
                start(sum_copy(sums_out.at[it, q, k], len(FIRST_SUMS) + k, i))

        def step_mean():
            total = pair_unit(chip)[...]
            for k in range(len(MERGED), CHIPS - 1):
                sum_copy(sums_in.at[it, q, k], k, 1).wait_recv()
                total = total + sums_in[it, q, k]
            tmpl[it, rows_of((2 * q + core) * HALF + chip * UNIT, UNIT), :] = total * (1.0 / FRAMES)
            for k, offset in enumerate(MEANS):
                start(mean_copy(0, k, offset))

        def step_pass():
            for k, (i, offset) in enumerate(PASSED):
                mean_copy(i, k, 1).wait_recv()
                start(mean_copy(i, len(MEANS) + k, offset))

        def step_share():
            for k, i in enumerate(LAST_MEANS):
                mean_copy(i, len(PASSED) + k, 1).wait_recv()
            start(to_mate(core))

        def step_end():
            to_mate(1 - core).wait_recv()

        steps = [step_swap, step_pair, step_merge, step_mean, step_pass, step_share, step_end]
        return [step for step in steps if (MERGED or step is not step_merge) and (PASSED or step is not step_pass)]

    def whiten(f_re, f_im, t_re, t_im):
        p_re = f_re * t_re + f_im * t_im
        p_im = f_im * t_re - f_re * t_im
        scale = lax.rsqrt(jnp.maximum(p_re * p_re + p_im * p_im, FLOOR * FLOOR))
        return p_re * scale, p_im * scale

    def halves(value):
        return value[:Z], value[Z:]

    def slot_of(ref, first, j):
        return halves(first[...] if j == 0 else ref[slot_rows(j), :])

    def packed(first, last):
        (f_re, f_im), (l_re, l_im) = first, last
        return jnp.concatenate([f_re - l_im, f_im + l_re], axis=0)

    def flipped(value):
        high, low = split(value)
        value = dot(flip_z[...], high) + dot(flip_z[...], low)
        high, low = split(part_rows(value))
        return halves(dot(high, flip_y[...]) + dot(low, flip_y[...]))

    def unpack(it):
        value = tmpl[it, slot_rows(0), :]
        re, im = halves(value)
        flip_re, flip_im = flipped(complex_rows(value))
        half = 0.5 * owner
        first_t[it] = jnp.concatenate([re - half * (re - flip_re), im - half * (im + flip_im)], axis=0)
        last_t[it] = jnp.concatenate([half * (im + flip_im), half * (flip_re - re)], axis=0)

    def back(values):
        lines = [jnp.concatenate([re, im], axis=1) for re, im in values]
        lines = dot_y(jnp.concatenate(lines, axis=0), iy)
        planes = [part_rows(lines[i * Z : (i + 1) * Z]) for i in range(len(values))]
        return z_dot(iz[...], jnp.concatenate(planes, axis=1))

    def inverse_part(n, q, slot_values, last_values):
        if q == 0:
            last = back([last_values()])
            last = jnp.concatenate([last[2 * Z - SLABS :], last[: 2 * Z - SLABS]], axis=0)

        for group in groups(q):
            planes = back([slot_values(j) for j in group])
            for k, j in enumerate(group):
                value = planes[:, k * 128 : (k + 1) * 128]
                if j == 0:
                    keep = jnp.where(first_part, 1.0, 1.0 - owner)
                    value = value * keep + last * (1.0 - keep)
                for d in range(SPACE):
                    send_i[n, rows_of(d * MSG + j * 8, 8), :] = value[8 * d : 8 * d + 8]
        exchange_part(send_i.at[n], recv_i.at[n], inv_send.at[n], inv_recv.at[n], q, by_part)

    def store_planes(z):
        planes = pl.ds(z, 2)
        return pltpu.make_async_copy(out_ref.at[planes], out_hbm.at[planes], out_sem.at[z // 2])

    def inverse_x(n, target):
        count = ROWS // 16

        def wait_one(q, carry):
            wait_part(send_i.at[n], recv_i.at[n], inv_send.at[n], inv_recv.at[n], q, by_part)
            return carry

        for half in range(2):
            lax.fori_loop(half * (NQ // 2), (half + 1) * (NQ // 2), wait_one, 0)
            for z in range(0, SLABS, 2):
                columns = []
                for i in range(2):
                    parts = [
                        recv_i[n, pl.ds(half * count * 8 + part * SLABS + z + i, count, stride=8), :]
                        for part in range(2)
                    ]
                    columns.append(jnp.concatenate(parts, axis=0))
                value = x_dot(ix[half], jnp.concatenate(columns, axis=1))
                for i in range(2):
                    plane = value[:, i * 128 : (i + 1) * 128]
                    target[z + i] = plane if half == 0 else target[z + i] + plane
                if half == 1 and n == ITERS:
                    store_planes(z).start()

    lane = lax.broadcasted_iota(jnp.int32, (1, 128), 1)

    def centroid(it):
        top = jnp.full((8, 128), -jnp.inf, F32)
        inverse_x(it, scores)
        for z in range(SLABS):
            top = jnp.maximum(top, jnp.max(scores[z].reshape(X // 8, 8, 128), axis=0))
        top = top * (SHARPNESS * NORM)
        top = jnp.max(jnp.max(top, axis=0, keepdims=True), axis=1, keepdims=True)
        step = 128
        x_row = lax.broadcasted_iota(jnp.int32, (step, 128), 0)
        zero = jnp.zeros((8, 128), F32)

        def weigh(i, carry):
            total, by_z, by_x = carry
            z, x = i // (X // step), (i % (X // step)) * step
            weights = jnp.exp(scores[z, rows_of(x, step), :] * (SHARPNESS * NORM) - top)
            x_at = ((x + x_row + X // 2) % X - X // 2).astype(F32)
            z_at = ((s * SLABS + z + Z // 2) % Z - Z // 2).astype(F32)
            here = jnp.sum(weights.reshape(step // 8, 8, 128), axis=0)
            by_x = by_x + jnp.sum((weights * x_at).reshape(step // 8, 8, 128), axis=0)
            return total + here, by_z + here * z_at, by_x

        total, by_z, by_x = lax.fori_loop(0, SLABS * X // step, weigh, (zero, zero, zero))
        y_at = ((lane + Y // 2) % Y - Y // 2).astype(F32)
        sums = [jnp.sum(value, axis=0, keepdims=True) for value in (total, by_z, by_x)]
        rows = [jnp.broadcast_to(top, (1, 128))] + sums + [sums[0] * y_at, jnp.zeros((3, 128), F32)]
        tile = jnp.concatenate(rows, axis=0)
        stats_out[it] = tile
        stats_in[it, s] = tile

        def stat(i, target, sender):
            d = (s + i) % SPACE
            return pltpu.make_async_remote_copy(
                src_ref=stats_out.at[it],
                dst_ref=stats_in.at[it, s if sender else d],
                send_sem=st_send.at[it, d],
                recv_sem=st_recv.at[it, s if sender else d],
                device_id={"space": d},
                device_id_type=MESH,
            )

        def send(i, carry):
            stat(i, s, True).start()
            return carry

        def receive(i, carry):
            stat(i, s, False).wait_recv()
            return carry

        lax.fori_loop(1, SPACE, send, 0)
        lax.fori_loop(1, SPACE, receive, 0)
        every = stats_in[it]
        tops = every[:, 0:1, :]
        scale = jnp.exp(tops - jnp.max(tops, axis=0, keepdims=True))
        sums = jnp.sum(jnp.sum(every * scale, axis=0), axis=1, keepdims=True)
        return [sums[i : i + 1] / sums[1:2] for i in (2, 3, 4)]

    def make_ramp(shifts):
        by_z, by_x, by_y = shifts
        kz = lax.broadcasted_iota(jnp.int32, (Z, 128), 0)
        ky = lax.broadcasted_iota(jnp.int32, (Z, 128), 1)
        phase = (2.0 * math.pi) * (signed(kz, Z) * (by_z / Z) + signed(ky, Y) * (by_y / Y))
        ramp_zy[0] = jnp.cos(phase)
        ramp_zy[1] = jnp.sin(phase)
        kx = s * SLOTS + lax.broadcasted_iota(jnp.int32, (SLOTS, 128), 0)
        phase = (2.0 * math.pi) * (kx.astype(F32) * (by_x / X))
        cos_x, sin_x = jnp.cos(phase), jnp.sin(phase)
        for j in range(SLOTS):
            ramp_x[0, j] = jnp.broadcast_to(cos_x[j : j + 1], (8, 128))
            ramp_x[1, j] = jnp.broadcast_to(sin_x[j : j + 1], (8, 128))

    def shifted_slot(j):
        cos_x = jnp.concatenate([ramp_x[0, j]] * (Z // 8), axis=0)
        sin_x = jnp.concatenate([ramp_x[1, j]] * (Z // 8), axis=0)
        cosine = ramp_zy[0] * cos_x - ramp_zy[1] * sin_x
        sine = ramp_zy[1] * cos_x + ramp_zy[0] * sin_x
        f_re, f_im = slot_of(spec, first_f, j)
        return f_re * cosine - f_im * sine, f_re * sine + f_im * cosine

    def shifted_last():
        f_re, f_im = halves(last_f[...])
        return f_re * ramp_zy[0] - f_im * ramp_zy[1], f_re * ramp_zy[1] + f_im * ramp_zy[0]

    def shift_part(q):
        for group in groups(q):
            for j in group:
                moved[slot_rows(j), :] = jnp.concatenate(shifted_slot(j), axis=0)
        if q == 0:
            moved[slot_rows(0), :] = packed(halves(moved[slot_rows(0), :]), shifted_last())

    for it in range(ITERS):

        def part_steps(q):
            def begin():
                if it == 0:
                    forward_part(q)
                else:
                    shift_part(q)

            def end():
                if q == 0:
                    unpack(it)
                inverse_part(
                    it,
                    q,
                    lambda j: whiten(*slot_of(spec, first_f, j), *slot_of(tmpl.at[it], first_t.at[it], j)),
                    lambda: whiten(*halves(last_f[...]), *halves(last_t[it])),
                )

            steps = sum_steps(it, q, moved if it > 0 else spec)
            return [lambda: (begin(), steps[0]())] + steps[1:-1] + [lambda: (steps[-1](), end())]

        plan = [
            (SPACING[it] * q + STEP * k, q, step) for q in range(NQ) for k, step in enumerate(part_steps(q))
        ]
        for _, _, step in sorted(plan, key=lambda entry: entry[:2]):
            step()
        shifts = centroid(it)
        make_ramp(shifts)

    for q in (1, 0, *range(2, NQ)):
        inverse_part(ITERS, q, shifted_slot, shifted_last)
    inverse_x(ITERS, out_ref)
    by_z, by_x, by_y = shifts
    line = jnp.where(lane == 0, by_z, jnp.where(lane == 1, by_x, by_y))
    shift_ref[...] = line[:, 0:3]

    for copy in sends:
        copy.wait_send()
    for z in range(0, SLABS, 2):
        store_planes(z).wait()

    def finish(q, carry):
        wait_sent(send_f, recv_f, fwd_send, fwd_recv, q, by_device)
        for n in range(ITERS + 1):
            wait_sent(send_i.at[n], recv_i.at[n], inv_send.at[n], inv_recv.at[n], q, by_part)
        return carry

    lax.fori_loop(0, NQ, finish, 0)
    for it in range(ITERS):

        def done(i, carry):
            d = (s + i) % SPACE
            pltpu.make_async_remote_copy(
                src_ref=stats_out.at[it],
                dst_ref=stats_in.at[it, s],
                send_sem=st_send.at[it, d],
                recv_sem=st_recv.at[it, s],
                device_id={"space": d},
                device_id_type=MESH,
            ).wait_send()
            return carry

        lax.fori_loop(1, SPACE, done, 0)


def body(volumes):
    consts = [jnp.asarray(table) for table in tables()]
    vmem = pl.BlockSpec(memory_space=pltpu.VMEM)
    hbm = pl.BlockSpec(memory_space=pltpu.HBM)
    dma = pltpu.SemaphoreType.DMA
    slots = SLOTS * 2 * Z
    corrected, shifts = pl.pallas_call(
        kernel,
        out_shape=(
            jax.ShapeDtypeStruct((SLABS, X, Y), F32),
            jax.ShapeDtypeStruct((1, 3), F32),
        ),
        in_specs=[hbm] * (1 + len(consts)),
        out_specs=(hbm, vmem),
        scratch_shapes=[
            pltpu.VMEM((SLABS, X, Y), F32),
            *[pltpu.VMEM(table.shape, BF16) for table in consts],
            pltpu.VMEM((SLABS, X, Y), F32),
            dma((SLABS // 2,)),
            pltpu.VMEM((ROWS, 128), F32),
            pltpu.VMEM((ROWS, 128), F32),
            pltpu.VMEM((slots, 128), F32),
            pltpu.VMEM((slots, 128), F32),
            pltpu.VMEM((2 * Z, 128), F32),
            pltpu.VMEM((2 * Z, 128), F32),
            pltpu.VMEM((ITERS, 2 * Z, 128), F32),
            pltpu.VMEM((ITERS, 2 * Z, 128), F32),
            pltpu.VMEM((ITERS, NQ, HALF, 128), F32),
            pltpu.VMEM((ITERS, NQ, HALF, 128), F32),
            pltpu.VMEM((ITERS, NQ, 7, UNIT, 128), F32),
            pltpu.VMEM((ITERS, NQ, 3, UNIT, 128), F32),
            pltpu.VMEM((ITERS, slots, 128), F32),
            pltpu.VMEM((ITERS + 1, ROWS, 128), F32),
            pltpu.VMEM((ITERS + 1, ROWS, 128), F32),
            pltpu.VMEM((SLABS, X, 128), F32),
            pltpu.VMEM((ITERS, 8, 128), F32),
            pltpu.VMEM((ITERS, SPACE, 8, 128), F32),
            pltpu.VMEM((2, Z, 128), F32),
            pltpu.VMEM((2, SLOTS, 8, 128), F32),
            dma((1 + len(consts),)),
            dma((NQ, SPACE)), dma((NQ, SPACE)),
            dma((ITERS + 1, NQ, SPACE)), dma((ITERS + 1, NQ, SPACE)),
            dma((ITERS, SPACE)), dma((ITERS, SPACE)),
            dma((ITERS, NQ)), dma((ITERS, NQ)),
            dma((ITERS, NQ, 7)), dma((ITERS, NQ, 7)),
            dma((ITERS, NQ, 7)), dma((ITERS, NQ, 7)),
            dma((ITERS, NQ)), dma((ITERS, NQ)),
        ],
        compiler_params=pltpu.CompilerParams(
            collective_id=0, has_side_effects=True, vmem_limit_bytes=56 * 2**20
        ),
        name="register",
    )(volumes[0], *consts)
    return corrected[None] * NORM, shifts


def solution(mesh):
    in_specs = (P("tm", "space", None, None),)
    out_specs = (P("tm", "space", None, None), P("tm", None))
    return jax.shard_map(body, mesh=mesh, in_specs=in_specs, out_specs=out_specs, check_vma=False)
```
